128 devices in a mesh: batch: 4 (over x_lo, core), patch: 32 (over y, z, x_hi).
Axes of the slice: x: 4 (x_hi: 2, x_lo: 2; x = x_hi * 2 + x_lo), y: 4, z: 4, core: 2. Of those that a mesh axis runs over, the one named last changes fastest.
Arguments:
- latent: bfloat16 [512, 64, 1280], P(('batch', 'patch')), parts along dimension 0, may hold values from -30 to 30
- gn_gain: float32 [1280], replicated, may hold values from 0.1 to 1.9
- w_query: bfloat16 [1280, 640], replicated, may hold values from -0.15625 to 0.15625
- w_key: bfloat16 [1280, 640], replicated, may hold values from -0.15625 to 0.15625
- w_value: bfloat16 [1280, 640], replicated, may hold values from -0.15625 to 0.15625
- w_out: bfloat16 [640, 1280], replicated, may hold values from -0.25 to 0.25
- stale_keys: bfloat16 [32768, 640], P(('batch', 'patch')), parts along dimension 0, may hold values from -150 to 150
- stale_values: bfloat16 [32768, 640], P(('batch', 'patch')), parts along dimension 0, may hold values from -5 to 5
- gn2_gain: float32 [1280], replicated, may hold values from 0.1 to 1.9
- conv_weight: bfloat16 [9, 1280, 640], replicated, may hold values from -0.0546875 to 0.0546875
- time_shift: float32 [2560], P('batch'), parts along dimension 0, may hold values from -4 to 4
Outputs:
- result: bfloat16 [512, 64, 640], P(('batch', 'patch')), parts along dimension 0
- fresh_keys: bfloat16 [32768, 640], P(('batch', 'patch')), parts along dimension 0
- fresh_values: bfloat16 [32768, 640], P(('batch', 'patch')), parts along dimension 0
The draws below stay inside these ranges and needn't reach their ends.
There are 4 independent parts, one for each index of `batch`. The reference program is written for one: setup_inputs(seed, part) draws one part's arguments, and reference() takes and returns one part's arrays. A program takes and returns all parts, laid end to end along the dimension named above; an argument that names none is the same for every part. Nothing has to cross between parts.
All inputs are finite; a program needn't handle non-finite values.
Results may differ from the reference program's by a relative error of at most 0.005.
The reference program's roundings to bfloat16 on the way count: a program that leaves them out, or rounds other values in their place, can miss the bound.
Values may be sent and summed in bfloat16 or wider, within the bound.
No kernel may reach another device: no remote copies, remote signals or barrier semaphores. Data moves between devices by JAX's collectives and lax.ppermute only.
A program may use at most 128 MiB of HBM per device.

```python
import math
import jax
import jax.numpy as jnp
from jax import lax

D = 1280
HEAD = 64
HEADS = 10
HALF = 640
GROUPS = 32
WIDE = 64
KV = 640
HEIGHT = 128
TOK_DEV = 256
TOKENS = 8192
N_PATCH = 32


def draw_latent(key, part):
    key = jax.random.fold_in(key, 11)
    first, second, third = jax.random.split(key, 3)
    noise = jnp.clip(jax.random.normal(first, (HEIGHT, WIDE, D), jnp.float32), -5.0, 5.0)
    rise = jnp.exp(math.log(3.0) * jnp.arange(HEIGHT, dtype=jnp.float32) / max(HEIGHT - 1, 1))[:, None, None]
    row_scale = jnp.exp(jax.random.uniform(second, (HEIGHT, 1, 1), jnp.float32) * math.log(2.0))
    chan_scale = jnp.exp(jax.random.uniform(third, (1, 1, D), jnp.float32) * math.log(4.0))
    return (0.25 * noise * rise * row_scale * chan_scale).astype(jnp.bfloat16)


def draw_stale_keys(key, part):
    key = jax.random.fold_in(key, 12)
    first = jax.random.fold_in(key, 0)
    noise = jnp.clip(jax.random.normal(first, (TOKENS, KV), jnp.float32), -5.0, 5.0)
    return noise.astype(jnp.bfloat16)


def shard_levels(key, shape, shards, low, top_value):
    def one(dim, blocks):
        heights = jax.random.uniform(jax.random.fold_in(jax.random.fold_in(key, 6), dim), (blocks,), jnp.float32, low / len(shards), top_value / len(shards))
        return jnp.repeat(jnp.exp(heights), shape[dim] // blocks).reshape((-1,) + (1,) * (len(shape) - dim - 1))

    loudness = one(*shards[0])
    for cut in shards[1:]:
        loudness = loudness * one(*cut)
    return loudness


def scatter_about(own_key, shape, scale, limit, shards=(), kind=jnp.bfloat16):
    entries = scale * jax.random.normal(own_key, shape, jnp.float32)
    if shards:
        entries = entries * shard_levels(own_key, shape, shards, -0.22, 0.18)
    return jnp.clip(entries, -limit, limit).astype(kind)


def setup_inputs(seed: int = 0, part: int = 0) -> dict:
    arg_keys = jax.random.split(jax.random.key(seed), 12)
    own_keys = jax.random.split(jax.random.fold_in(arg_keys[11], part), 12)
    return {
        "latent": draw_latent(jax.random.fold_in(jax.random.fold_in(arg_keys[11], part), 71), part),
        "gn_gain": jnp.clip(1.0 + 0.18 * jax.random.normal(arg_keys[1], (D,), jnp.float32), 0.1, 1.9),
        "w_query": scatter_about(arg_keys[2], (D, KV), D ** -0.5, 0.15625),
        "w_key": scatter_about(arg_keys[3], (D, KV), D ** -0.5, 0.15625),
        "w_value": scatter_about(arg_keys[4], (D, KV), D ** -0.5, 0.15625),
        "w_out": scatter_about(arg_keys[5], (KV, D), KV ** -0.5, 0.25),
        "stale_keys": draw_stale_keys(jax.random.fold_in(jax.random.fold_in(arg_keys[11], part), 71), part),
        "stale_values": scatter_about(own_keys[7], (TOKENS, KV), 1.0, 5.0, ((0, 32),)),
        "gn2_gain": jnp.clip(1.0 + 0.18 * jax.random.normal(arg_keys[8], (D,), jnp.float32), 0.1, 1.9),
        "conv_weight": scatter_about(arg_keys[9], (9, D, HALF), (9 * D) ** -0.5, 0.0546875),
        "time_shift": scatter_about(own_keys[10], (HALF,), 1.0, 4.0, (), jnp.float32),
    }


def group_norm(features, gain):
    grouped = features.reshape(-1, GROUPS, D // GROUPS)
    center = lax.optimization_barrier(jnp.mean(grouped, axis=(0, 2)))
    variance = lax.optimization_barrier(jnp.mean(jnp.square(grouped - center[None, :, None]), axis=(0, 2)))
    scaled = (grouped - center[None, :, None]) * lax.rsqrt(variance + 1e-05)[None, :, None]
    return scaled.reshape(features.shape) * gain

def reference(latent, gn_gain, w_query, w_key, w_value, w_out, stale_keys, stale_values, gn2_gain, conv_weight, time_shift):
    features = latent.astype(jnp.float32)
    normed = group_norm(features, gn_gain).astype(jnp.bfloat16).reshape(TOKENS, D)
    queries = jnp.dot(normed, w_query, preferred_element_type=jnp.float32).astype(jnp.bfloat16)
    fresh_keys = jnp.dot(normed, w_key, preferred_element_type=jnp.float32).astype(jnp.bfloat16)
    fresh_values = jnp.dot(normed, w_value, preferred_element_type=jnp.float32).astype(jnp.bfloat16)

    def band_attention(band_no):
        start = (band_no * TOK_DEV).astype(jnp.int32)
        query_rows = lax.dynamic_slice_in_dim(queries, start, TOK_DEV, 0).reshape(TOK_DEV, HEADS, HEAD).astype(jnp.float32)
        keys_all = lax.dynamic_update_slice_in_dim(stale_keys, lax.dynamic_slice_in_dim(fresh_keys, start, TOK_DEV, 0), start, 0)
        values_all = lax.dynamic_update_slice_in_dim(stale_values, lax.dynamic_slice_in_dim(fresh_values, start, TOK_DEV, 0), start, 0)
        scores = jnp.einsum('qhd,khd->qhk', query_rows, keys_all.reshape(TOKENS, HEADS, HEAD).astype(jnp.float32)) * 0.125
        top = lax.optimization_barrier(jnp.max(scores, axis=2))
        weights = jnp.exp(scores - top[..., None])
        total = lax.optimization_barrier(jnp.sum(weights, axis=2))
        rounded = lax.optimization_barrier(weights.astype(jnp.bfloat16)).astype(jnp.float32)
        summed = jnp.einsum('qhk,khd->qhd', rounded, values_all.reshape(TOKENS, HEADS, HEAD).astype(jnp.float32))
        return (summed / total[..., None]).astype(jnp.bfloat16).reshape(TOK_DEV, KV)
    attended = lax.map(band_attention, jnp.arange(N_PATCH, dtype=jnp.int32)).reshape(TOKENS, KV)
    mixed = jnp.dot(attended, w_out, preferred_element_type=jnp.float32).reshape(HEIGHT, WIDE, D)
    hidden = features + mixed
    activated = jax.nn.silu(group_norm(hidden, gn2_gain)).astype(jnp.bfloat16)
    padded = jnp.pad(activated, ((1, 1), (1, 1), (0, 0)))
    conv_sum = jnp.zeros((TOKENS, HALF), jnp.float32)
    for tap_row in range(3):
        for tap_col in range(3):
            window = padded[tap_row:tap_row + HEIGHT, tap_col:tap_col + WIDE].reshape(TOKENS, D)
            conv_sum = conv_sum + jnp.dot(window, conv_weight[3 * tap_row + tap_col], preferred_element_type=jnp.float32)
    result = hidden[..., :HALF] + conv_sum.reshape(HEIGHT, WIDE, HALF) + time_shift
    return (result.astype(jnp.bfloat16), fresh_keys, fresh_values)
```

```python
import functools

import jax
import jax.numpy as jnp
from jax import lax
from jax.experimental import pallas as pl
from jax.experimental.pallas import tpu as pltpu
from jax.sharding import PartitionSpec as P

HEAD = 64
GROUPS = 32
LANES = 128
NY, NZ, NX = 4, 4, 2
EPS = 1e-05
BF = jnp.bfloat16
F32 = jnp.float32
EXACT = lax.Precision.HIGHEST


def shifted(x, dy, dz, dx):
    pairs = []
    for y in range(NY):
        for z in range(NZ):
            for c in range(NX):
                to = (((y + dy) % NY) * NZ + (z + dz) % NZ) * NX + (c + dx) % NX
                pairs.append(((y * NZ + z) * NX + c, to))
    return lax.ppermute(x, "patch", pairs)


def members_of(channels, lead, offset):
    width = channels // GROUPS
    shape = (channels, LANES) if lead else (LANES, channels)
    chan = lax.broadcasted_iota(jnp.int32, shape, 0 if lead else 1)
    group = lax.broadcasted_iota(jnp.int32, shape, 1 if lead else 0) - offset
    inside = (chan >= group * width) & (chan < group * width + width)
    return jnp.where(inside, 1.0, 0.0).astype(F32)


def exact_dot(a, b):
    return jnp.dot(a, b, preferred_element_type=F32, precision=EXACT)


def local_stats(x, peers):
    rows, channels = x.shape
    count = rows * (channels // GROUPS)
    total = jnp.sum(x, axis=0, keepdims=True)
    mean = exact_dot(jnp.broadcast_to(total, (8, channels)), members_of(channels, True, 0)) / count
    center = exact_dot(mean, members_of(channels, False, 0))
    squares = jnp.sum(jnp.square(x - center[:1]), axis=0, keepdims=True)
    spread = exact_dot(
        jnp.broadcast_to(squares, (8, channels)), members_of(channels, True, GROUPS)
    )
    return jnp.broadcast_to((mean + spread)[:1], (peers, LANES))


def combined(stats, channels, count):
    peers = stats.shape[0]
    total = jnp.sum(stats, axis=0, keepdims=True)
    mean = total / peers
    between = jnp.sum(jnp.square(stats - mean), axis=0, keepdims=True) * count
    lead = members_of(channels, False, 0)
    eight = lambda v: jnp.broadcast_to(v, (8, LANES))
    center = exact_dot(eight(mean), lead)[:1]
    spread = exact_dot(eight(between), lead) + exact_dot(
        eight(total), members_of(channels, False, GROUPS)
    )
    return center, lax.rsqrt(spread[:1] / (count * peers) + EPS)


def full(shape):
    return pl.BlockSpec(shape, lambda *_: (0,) * len(shape))


def stats_kernel(x_ref, out_ref):
    out_ref[...] = local_stats(x_ref[...].astype(F32), out_ref.shape[0])


def norm_stats(x, peers):
    return pl.pallas_call(
        stats_kernel,
        out_shape=jax.ShapeDtypeStruct((peers, LANES), F32),
        name="norm_stats",
        cost_estimate=pl.CostEstimate(flops=4 * x.size, bytes_accessed=2 * x.size, transcendentals=0),
    )(x)


def project_kernel(stats_ref, x_ref, gain_ref, wq_ref, wk_ref, wv_ref, q_ref, k_ref, v_ref):
    rows, channels = x_ref.shape
    center, scale = combined(stats_ref[...], channels, rows * (channels // GROUPS))
    normed = ((x_ref[...].astype(F32) - center) * scale * gain_ref[...]).astype(BF)
    for w_ref, o_ref in ((wq_ref, q_ref), (wk_ref, k_ref), (wv_ref, v_ref)):
        o_ref[...] = jnp.dot(normed, w_ref[...], preferred_element_type=F32).astype(BF)


def project(stats, x, gain, wq, wk, wv):
    rows, channels = x.shape
    width = wq.shape[1]
    return pl.pallas_call(
        project_kernel,
        out_shape=[jax.ShapeDtypeStruct((rows, width), BF)] * 3,
        name="project",
        compiler_params=pltpu.CompilerParams(vmem_limit_bytes=24 * 2**20),
        cost_estimate=pl.CostEstimate(
            flops=6 * rows * channels * width,
            bytes_accessed=6 * channels * width,
            transcendentals=0,
        ),
    )(stats, x, gain, wq, wk, wv)


def attend_pair(queries, keys, values):
    rows = queries.shape[0]
    first = lax.broadcasted_iota(jnp.int32, (rows, LANES), 1) < HEAD
    scaled = queries * BF(0.125)
    none = jnp.zeros_like(scaled)
    found = []
    for mine in (jnp.where(first, scaled, none), jnp.where(first, none, scaled)):
        scores = lax.dot_general(
            mine, keys, (((1,), (1,)), ((), ())), preferred_element_type=F32
        )
        top = jnp.max(scores, axis=1, keepdims=True)
        weights = jnp.exp(scores - top).astype(BF)
        both = jnp.dot(weights, values, preferred_element_type=F32)
        found.append((both[:, :LANES], jnp.broadcast_to(top, (rows, LANES)), both[:, LANES:]))
    return first, found


def near_kernel(
    q0, q1, q2, q3, fresh_k, fresh_v, old_k, old_v, a_ref, b_ref, c_ref, sum_ref, top_ref, tot_ref, keys, values
):
    rows = q0.shape[0]
    keys[0:rows, :] = fresh_k[...]
    values[0:rows, 0:LANES] = fresh_v[...]
    for i, ref in enumerate((a_ref, b_ref, c_ref)):
        at = slice((i + 1) * rows, (i + 2) * rows)
        keys[at, :] = ref[0:rows, :]
        values[at, 0:LANES] = ref[rows : 2 * rows, :]
    keys[4 * rows : 5 * rows, :] = old_k[...]
    values[4 * rows : 5 * rows, 0:LANES] = old_v[...]
    values[:, LANES:] = jnp.ones((5 * rows, LANES), BF)
    for band, q_ref in enumerate((q0, q1, q2, q3)):
        span = slice(0, 4 * rows) if band == 0 else slice(rows, 5 * rows)
        first, found = attend_pair(q_ref[...], keys[span, :], values[span, :])
        at = slice(band * rows, (band + 1) * rows)
        for which, out_ref in enumerate((sum_ref, top_ref, tot_ref)):
            out_ref[at, :] = jnp.where(first, found[0][which], found[1][which])


def near_attention(queries, fresh, old, blocks):
    rows, width = queries[0].shape
    pairs = width // LANES
    one = pl.BlockSpec((rows, LANES), lambda j: (0, j))
    two = pl.BlockSpec((2 * rows, LANES), lambda j: (0, j))
    four = pl.BlockSpec((4 * rows, LANES), lambda j: (0, j))
    return pl.pallas_call(
        near_kernel,
        grid=(pairs,),
        in_specs=[one] * 8 + [two] * 3,
        out_specs=[four] * 3,
        out_shape=[jax.ShapeDtypeStruct((4 * rows, width), F32)] * 3,
        scratch_shapes=[pltpu.VMEM((5 * rows, LANES), BF), pltpu.VMEM((5 * rows, 2 * LANES), BF)],
        name="near_attention",
        compiler_params=pltpu.CompilerParams(vmem_limit_bytes=32 * 2**20),
        cost_estimate=pl.CostEstimate(
            flops=64 * rows * rows * width, bytes_accessed=40 * rows * width, transcendentals=0
        ),
    )(*queries, *fresh, *old, *blocks)


def far_kernel(
    q0, q1, q2, q3, a_ref, b_ref, kk_ref, vv_ref, sum_ref, top_ref, tot_ref, o0, o1, o2, o3, keys, values
):
    rows = q0.shape[0]
    j = pl.program_id(0)
    for i, ref in enumerate((a_ref, b_ref)):
        at = slice(i * rows, (i + 1) * rows)
        keys[at, :] = ref[0:rows, :]
        values[at, 0:LANES] = ref[rows : 2 * rows, :]
    keys[2 * rows : 4 * rows, :] = kk_ref[...]
    values[2 * rows : 4 * rows, 0:LANES] = vv_ref[...]
    values[:, LANES:] = jnp.ones((4 * rows, LANES), BF)
    lane = lax.broadcasted_iota(jnp.int32, (rows, LANES), 1)
    width = 5 * LANES
    for band, (q_ref, o_ref) in enumerate(((q0, o0), (q1, o1), (q2, o2), (q3, o3))):
        first, found = attend_pair(q_ref[...], keys[...], values[...])
        at = slice(band * rows, (band + 1) * rows)
        pick = lambda n: jnp.where(first, found[0][n], found[1][n])
        far_top, near_top = pick(1), top_ref[at, :]
        top = jnp.maximum(far_top, near_top)
        far_part, near_part = jnp.exp(far_top - top), jnp.exp(near_top - top)
        total = far_part * pick(2) + near_part * tot_ref[at, :]
        summed = far_part * pick(0) + near_part * sum_ref[at, :]
        o_ref[:, pl.ds(pl.multiple_of(j * LANES, LANES), LANES)] = (summed / total).astype(BF)
        level = top + jnp.log(total)
        swapped = pltpu.roll(level, HEAD, 1)
        row_level = (jnp.where(first, level, swapped), jnp.where(first, swapped, level))
        extra = jnp.where(j == 0, jnp.zeros((rows, LANES), BF), o_ref[:, width:])
        for h in range(2):
            rest = row_level[h]
            for piece in range(3):
                part = rest.astype(BF)
                rest = rest - part.astype(F32)
                extra = jnp.where(lane == 2 * j + h + 10 * piece, part, extra)
        o_ref[:, width:] = extra


def far_attention(queries, blocks, kk, vv, state):
    rows, width = queries[0].shape
    pairs = width // LANES
    one = pl.BlockSpec((rows, LANES), lambda j: (0, j))
    two = pl.BlockSpec((2 * rows, LANES), lambda j: (0, j))
    four = pl.BlockSpec((4 * rows, LANES), lambda j: (0, j))
    wide = width + LANES
    return pl.pallas_call(
        far_kernel,
        grid=(pairs,),
        in_specs=[one] * 4 + [two] * 4 + [four] * 3,
        out_specs=[full((rows, wide))] * 4,
        out_shape=[jax.ShapeDtypeStruct((rows, wide), BF)] * 4,
        scratch_shapes=[pltpu.VMEM((4 * rows, LANES), BF), pltpu.VMEM((4 * rows, 2 * LANES), BF)],
        name="far_attention",
        compiler_params=pltpu.CompilerParams(vmem_limit_bytes=32 * 2**20),
        cost_estimate=pl.CostEstimate(
            flops=64 * rows * rows * width, bytes_accessed=40 * rows * width, transcendentals=0
        ),
    )(*queries, *blocks, kk, vv, *state)


def merge_kernel(p0, p1, p2, p3, x_ref, w_ref, hidden_ref, stats_ref):
    width = w_ref.shape[0]
    lane = lax.broadcasted_iota(jnp.int32, (LANES, width), 0)
    chan = lax.broadcasted_iota(jnp.int32, (LANES, width), 1)
    spread = jnp.zeros((LANES, width), F32)
    for piece in range(3):
        head = lane - 10 * piece
        inside = (head >= 0) & (head < 10) & (chan >= head * HEAD) & (chan < head * HEAD + HEAD)
        spread = jnp.where(inside, 1.0, spread)
    spread = spread.astype(BF)
    parts = (p0, p1, p2, p3)
    levels = [jnp.dot(p[:, width:], spread, preferred_element_type=F32) for p in parts]
    top = functools.reduce(jnp.maximum, levels)
    shares = [jnp.exp(level - top) for level in levels]
    total = functools.reduce(jnp.add, shares)
    summed = functools.reduce(
        jnp.add, [s * p[:, :width].astype(F32) for s, p in zip(shares, parts)]
    )
    attended = (summed / total).astype(BF)
    hidden = x_ref[...].astype(F32) + jnp.dot(attended, w_ref[...], preferred_element_type=F32)
    hidden_ref[...] = hidden
    stats_ref[...] = local_stats(hidden, stats_ref.shape[0])


def merge(parts, x, w_out, peers):
    rows, channels = x.shape
    return pl.pallas_call(
        merge_kernel,
        out_shape=[
            jax.ShapeDtypeStruct((rows, channels), F32),
            jax.ShapeDtypeStruct((peers, LANES), F32),
        ],
        name="merge_project",
        compiler_params=pltpu.CompilerParams(vmem_limit_bytes=24 * 2**20),
        cost_estimate=pl.CostEstimate(
            flops=2 * rows * w_out.size, bytes_accessed=2 * w_out.size, transcendentals=0
        ),
    )(*parts, x, w_out)


def conv_kernel(
    edge_ref, stats_ref, hidden_ref, above_ref, below_ref, gain_ref, w_ref, shift_ref, out_ref, moved, total, cols
):
    tap = pl.program_id(0)
    rows, channels = hidden_ref.shape
    width = out_ref.shape[1]

    @pl.when(tap == 0)
    def _():
        center, scale = combined(stats_ref[...], channels, rows * (channels // GROUPS))
        pieces = (
            (above_ref, 0, cols, edge_ref[0] == 0),
            (hidden_ref, cols, rows, None),
            (below_ref, cols + rows, cols, edge_ref[1] == 0),
        )
        for ref, start, size, kept in pieces:
            for part in range(size // cols):
                at = slice(part * cols, (part + 1) * cols)
                v = (ref[at, :] - center) * scale * gain_ref[...]
                v = v / (1.0 + jnp.exp(-v))
                if kept is not None:
                    v = jnp.where(kept, v, 0.0)
                col = lax.broadcasted_iota(jnp.int32, (cols, channels), 0)
                to = slice(start + part * cols, start + (part + 1) * cols)
                moved[1, to, :] = v.astype(BF)
                moved[0, to, :] = jnp.where(col == 0, 0.0, pltpu.roll(v, 1, 0)).astype(BF)
                moved[2, to, :] = jnp.where(col == cols - 1, 0.0, pltpu.roll(v, cols - 1, 0)).astype(BF)
        total[...] = hidden_ref[:, :width] + shift_ref[...]

    row = lax.div(tap, 3)
    window = moved[lax.rem(tap, 3), pl.ds(pl.multiple_of(row * cols, cols), rows), :]
    total[...] += jnp.dot(window, w_ref[0], preferred_element_type=F32)

    @pl.when(tap == pl.num_programs(0) - 1)
    def _():
        out_ref[...] = total[...].astype(BF)


def convolve(edges, stats, hidden, above, below, gain, weight, shift):
    rows, channels = hidden.shape
    cols = above.shape[0]
    width = weight.shape[2]
    return pl.pallas_call(
        functools.partial(conv_kernel, cols=cols),
        grid=(9,),
        in_specs=[
            pl.BlockSpec(memory_space=pltpu.SMEM),
            full(stats.shape),
            full(hidden.shape),
            full(above.shape),
            full(below.shape),
            full(gain.shape),
            pl.BlockSpec((1, channels, width), lambda t: (t, 0, 0)),
            full(shift.shape),
        ],
        out_specs=full((rows, width)),
        out_shape=jax.ShapeDtypeStruct((rows, width), BF),
        scratch_shapes=[
            pltpu.VMEM((3, rows + 2 * cols, channels), BF),
            pltpu.VMEM((rows, width), F32),
        ],
        name="norm_convolve",
        compiler_params=pltpu.CompilerParams(vmem_limit_bytes=32 * 2**20),
        cost_estimate=pl.CostEstimate(
            flops=2 * rows * weight.size, bytes_accessed=2 * weight.size, transcendentals=0
        ),
    )(edges, stats, hidden, above, below, gain, weight, shift)


def everyones(stats):
    return lax.all_to_all(stats, "patch", 0, 0, tiled=True)


def shards(
    latent,
    gn_gain,
    w_query,
    w_key,
    w_value,
    w_out,
    stale_keys,
    stale_values,
    gn2_gain,
    conv_weight,
    time_shift,
):
    row_count, col_count, channels = latent.shape
    tok_count = row_count * col_count
    peers = lax.axis_size("patch")
    own = lax.axis_index("patch")
    x = latent.reshape(tok_count, channels)
    old = jnp.concatenate([stale_keys, stale_values], axis=0)
    from_below = shifted(old, 1, 0, 0)
    from_above = shifted(old, -1, 0, 0)
    from_side = shifted(old, 0, 0, 1)

    stats = everyones(norm_stats(x, peers))
    queries, fresh_keys, fresh_values = project(
        stats, x, gn_gain.reshape(1, channels), w_query, w_key, w_value
    )
    side_below = shifted(from_side, 1, 0, 0)
    side_above = shifted(from_side, -1, 0, 0)
    bands = (
        queries,
        shifted(queries, 0, 1, 0),
        shifted(queries, 0, -1, 0),
        shifted(queries, 0, 2, 0),
    )
    last_keys = shifted(jnp.concatenate([from_below[:tok_count], side_below[:tok_count]]), 1, 0, 0)
    last_values = shifted(jnp.concatenate([from_above[tok_count:], side_above[tok_count:]]), -1, 0, 0)

    state = near_attention(
        bands,
        (fresh_keys, fresh_values),
        (stale_keys, stale_values),
        (from_below, from_above, from_side),
    )
    parts = far_attention(bands, (side_below, side_above), last_keys, last_values, state)
    parts = (
        parts[0],
        shifted(parts[1], 0, -1, 0),
        shifted(parts[2], 0, 1, 0),
        shifted(parts[3], 0, 2, 0),
    )
    hidden, stats = merge(parts, x, w_out, peers)
    down = [(i, i + 1) for i in range(peers - 1)]
    above = lax.ppermute(hidden[tok_count - col_count :], "patch", down)
    below = lax.ppermute(hidden[:col_count], "patch", [(j, i) for i, j in down])
    edges = jnp.stack([own == 0, own == peers - 1]).astype(jnp.int32)
    result = convolve(
        edges,
        everyones(stats),
        hidden,
        above,
        below,
        gn2_gain.reshape(1, channels),
        conv_weight,
        time_shift.reshape(1, -1),
    )
    return (result.reshape(row_count, col_count, -1), fresh_keys, fresh_values)


def solution(mesh):
    placed = (
        P(("batch", "patch"), None, None),
        P(),
        P(),
        P(),
        P(),
        P(),
        P(("batch", "patch"), None),
        P(("batch", "patch"), None),
        P(),
        P(),
        P("batch"),
    )
    return jax.shard_map(
        shards,
        mesh=mesh,
        in_specs=placed,
        out_specs=(
            P(("batch", "patch"), None, None),
            P(("batch", "patch"), None),
            P(("batch", "patch"), None),
        ),
        check_vma=False,
    )
```

```python
import functools

import jax
import jax.numpy as jnp
from jax import lax
from jax.experimental import pallas as pl
from jax.experimental.pallas import tpu as pltpu
from jax.sharding import PartitionSpec as P

HEAD = 64
GROUPS = 32
LANES = 128
NY, NZ, NX = 4, 4, 2
EPS = 1e-05
BF = jnp.bfloat16
F32 = jnp.float32


def shifted(x, dy, dz, dx):
    pairs = []
    for y in range(NY):
        for z in range(NZ):
            for c in range(NX):
                to = (((y + dy) % NY) * NZ + (z + dz) % NZ) * NX + (c + dx) % NX
                pairs.append(((y * NZ + z) * NX + c, to))
    return lax.ppermute(x, "patch", pairs)


def members_of(channels, lead, offset):
    width = channels // GROUPS
    shape = (channels, LANES) if lead else (LANES, channels)
    chan = lax.broadcasted_iota(jnp.int32, shape, 0 if lead else 1)
    group = lax.broadcasted_iota(jnp.int32, shape, 1 if lead else 0) - offset
    inside = (chan >= group * width) & (chan < group * width + width)
    return jnp.where(inside, 1.0, 0.0).astype(BF)


def exact_dot(row, ones):
    at = lax.broadcasted_iota(jnp.int32, (16, row.shape[1]), 0)
    rest, cut = row, jnp.zeros((16, row.shape[1]), F32)
    for piece in range(3):
        part = rest.astype(BF).astype(F32)
        rest = rest - part
        cut = jnp.where(at == piece, part, cut)
    return jnp.sum(
        jnp.dot(cut.astype(BF), ones, preferred_element_type=F32), axis=0, keepdims=True
    )


def local_stats(x, peers):
    rows, channels = x.shape
    count = rows * (channels // GROUPS)
    total = jnp.sum(x, axis=0, keepdims=True)
    mean = exact_dot(total, members_of(channels, True, 0)) / count
    center = exact_dot(mean, members_of(channels, False, 0))
    squares = jnp.sum(jnp.square(x - center), axis=0, keepdims=True)
    spread = exact_dot(squares, members_of(channels, True, GROUPS))
    return jnp.broadcast_to(mean + spread, (peers, LANES))


def combined(stats, channels, count):
    peers = stats.shape[0]
    total = jnp.sum(stats, axis=0, keepdims=True)
    mean = total / peers
    between = jnp.sum(jnp.square(stats - mean), axis=0, keepdims=True) * count
    lead = members_of(channels, False, 0)
    center = exact_dot(mean, lead)
    spread = exact_dot(between, lead) + exact_dot(total, members_of(channels, False, GROUPS))
    return center, lax.rsqrt(spread / (count * peers) + EPS)


def full(shape):
    return pl.BlockSpec(shape, lambda *_: (0,) * len(shape))


HBM = pl.BlockSpec(memory_space=pltpu.HBM)
VMEM = pl.BlockSpec(memory_space=pltpu.VMEM)


def halves(src, dst, sems, first):
    size = src.shape[0] // 2
    return [
        pltpu.make_async_copy(
            src.at[i * size : (i + 1) * size], dst.at[i * size : (i + 1) * size], sems.at[first + i]
        )
        for i in range(2)
    ]


def stats_kernel(x_ref, k_ref, v_ref, wq, wk, wv, out_ref, old_ref, wq_out, wk_out, wv_out, held, sems):
    rows = k_ref.shape[0]
    copies = halves(x_ref, held, sems, 0)
    copies.append(pltpu.make_async_copy(k_ref, old_ref.at[0:rows], sems.at[2]))
    copies.append(pltpu.make_async_copy(v_ref, old_ref.at[rows : 2 * rows], sems.at[3]))
    for i, (src, dst) in enumerate(((wq, wq_out), (wk, wk_out), (wv, wv_out))):
        copies += halves(src, dst, sems, 4 + 2 * i)
    for copy in copies:
        copy.start()
    for copy in copies[:2]:
        copy.wait()
    out_ref[...] = local_stats(held[...].astype(F32), out_ref.shape[0])
    for copy in copies[2:]:
        copy.wait()


def norm_stats(x, keys, values, weights, peers):
    rows, width = keys.shape
    return pl.pallas_call(
        stats_kernel,
        in_specs=[HBM] * 6,
        out_specs=[VMEM] * 5,
        out_shape=[
            jax.ShapeDtypeStruct((peers, LANES), F32),
            jax.ShapeDtypeStruct((2 * rows, width), BF),
        ]
        + [pltpu.VMEM(w.shape, w.dtype) for w in weights],
        scratch_shapes=[pltpu.VMEM(x.shape, x.dtype), pltpu.SemaphoreType.DMA((10,))],
        name="norm_stats",
        compiler_params=pltpu.CompilerParams(vmem_limit_bytes=60030976),
        cost_estimate=pl.CostEstimate(flops=4 * x.size, bytes_accessed=2 * x.size, transcendentals=0),
    )(x, keys, values, *weights)


def project_kernel(stats_ref, x_ref, gain_ref, wq, wk, wv, q_ref, k_ref, v_ref, both_ref):
    rows, channels = x_ref.shape
    center, scale = combined(stats_ref[...], channels, rows * (channels // GROUPS))
    gain = gain_ref[...].reshape(1, channels)
    normed = ((x_ref[...].astype(F32) - center) * scale * gain).astype(BF)
    for i, (w_ref, o_ref) in enumerate(((wq, q_ref), (wk, k_ref), (wv, v_ref))):
        found = jnp.dot(normed, w_ref[...], preferred_element_type=F32).astype(BF)
        o_ref[...] = found
        if i > 0:
            both_ref[(i - 1) * rows : i * rows, :] = found


def project(stats, x, gain, wq, wk, wv):
    rows, channels = x.shape
    width = wq.shape[1]
    return pl.pallas_call(
        project_kernel,
        in_specs=[VMEM] * 6,
        out_specs=[VMEM] * 4,
        out_shape=[jax.ShapeDtypeStruct((rows, width), BF)] * 3
        + [jax.ShapeDtypeStruct((2 * rows, width), BF)],
        name="project",
        compiler_params=pltpu.CompilerParams(vmem_limit_bytes=24 * 2**20),
        cost_estimate=pl.CostEstimate(
            flops=6 * rows * channels * width,
            bytes_accessed=6 * channels * width,
            transcendentals=0,
        ),
    )(stats, x, gain, wq, wk, wv)


def attend_pair(queries, keys, values):
    rows = queries.shape[0]
    first = lax.broadcasted_iota(jnp.int32, (rows, LANES), 1) < HEAD
    scaled = queries * BF(0.125)
    none = jnp.zeros_like(scaled)
    found = []
    for mine in (jnp.where(first, scaled, none), jnp.where(first, none, scaled)):
        scores = lax.dot_general(
            mine, keys, (((1,), (1,)), ((), ())), preferred_element_type=F32
        )
        top = jnp.max(scores, axis=1, keepdims=True)
        weights = jnp.exp(scores - top).astype(BF)
        both = jnp.dot(weights, values, preferred_element_type=F32)
        found.append((both[:, :LANES], jnp.broadcast_to(top, (rows, LANES)), both[:, LANES:]))
    return first, found


def attend_kernel(plan, start, final, waits, carry, *refs):
    count, rows_of = plan
    refs = list(refs)
    take = lambda n: [refs.pop(0) for _ in range(n)]
    queries, sources = take(count), take(2 * len(rows_of))
    state = take(3) if start else None
    take(waits)
    brought = take(1 if carry else 0)
    outs = take(count if final else 3)
    copies = []
    if carry:
        (kept,), (sems,) = take(1), take(1)
        copies = [
            pltpu.make_async_copy(brought[0].at[i], kept.at[i], sems.at[i]) for i in range(kept.shape[0])
        ]
        for copy in copies:
            copy.start()
    rows, width = queries[0].shape
    lane = lax.broadcasted_iota(jnp.int32, (rows, LANES), 1)
    ones = jnp.ones((rows, LANES), BF)
    extras = [jnp.zeros((rows, LANES), BF)] * count
    for j in range(width // LANES):
        cols = slice(j * LANES, (j + 1) * LANES)
        keys, values = [], []
        for i, (key_row, value_row) in enumerate(rows_of):
            keys.append(sources[2 * i][key_row * rows : (key_row + 1) * rows, cols])
            value = sources[2 * i + 1][value_row * rows : (value_row + 1) * rows, cols]
            values.append(jnp.concatenate([value, ones], axis=1))
        keys, values = jnp.concatenate(keys, axis=0), jnp.concatenate(values, axis=0)
        for band, q_ref in enumerate(queries):
            first, found = attend_pair(q_ref[:, cols], keys, values)
            at = slice(band * rows, (band + 1) * rows)
            summed, top, total = (jnp.where(first, found[0][n], found[1][n]) for n in range(3))
            if state is not None:
                old_top = state[1][at, cols]
                new_top = jnp.maximum(top, old_top)
                part, old_part = jnp.exp(top - new_top), jnp.exp(old_top - new_top)
                top = new_top
                total = part * total + old_part * state[2][at, cols]
                summed = part * summed + old_part * state[0][at, cols]
            if not final:
                for out_ref, value in zip(outs, (summed, top, total)):
                    out_ref[at, cols] = value
                continue
            outs[band][:, cols] = (summed / total).astype(BF)
            level = top + jnp.log(total)
            swapped = pltpu.roll(level, HEAD, 1)
            row_level = (jnp.where(first, level, swapped), jnp.where(first, swapped, level))
            for h in range(2):
                rest = row_level[h]
                for piece in range(3):
                    part = rest.astype(BF)
                    rest = rest - part.astype(F32)
                    extras[band] = jnp.where(lane == 2 * j + h + 10 * piece, part, extras[band])
    if final:
        for o_ref, extra in zip(outs, extras):
            o_ref[:, width : width + LANES] = extra
            if o_ref.shape[1] > width + LANES:
                o_ref[:, width + LANES :] = jnp.zeros((rows, o_ref.shape[1] - width - LANES), BF)
    for copy in copies:
        copy.wait()


def attend(name, queries, blocks, state=None, final=False, after=(), carry=None, weight=16, extra=1):
    rows, width = queries[0].shape
    count = len(queries)
    sources = []
    for keys, _, values, _ in blocks:
        sources += [keys, values]
    plan = (count, [(key_row, value_row) for _, key_row, _, value_row in blocks])
    if final:
        out_shape = [jax.ShapeDtypeStruct((rows, width + extra * LANES), BF)] * count
    else:
        out_shape = [jax.ShapeDtypeStruct((count * rows, width), F32)] * 3
    scratch, carried = [], []
    if carry is not None:
        out_shape.append(pltpu.VMEM(carry.shape, carry.dtype))
        scratch.append(pltpu.SemaphoreType.DMA((carry.shape[0],)))
        carried.append(carry)
    state = tuple(state or ())
    return pl.pallas_call(
        functools.partial(attend_kernel, plan, bool(state), final, len(after), carry is not None),
        in_specs=[VMEM] * (count + len(sources) + len(state))
        + [pl.BlockSpec(memory_space=pl.ANY)] * len(after)
        + [HBM] * len(carried),
        out_specs=[VMEM] * len(out_shape),
        out_shape=out_shape,
        scratch_shapes=scratch,
        name=name,
        compiler_params=pltpu.CompilerParams(vmem_limit_bytes=24 * 2**20),
        cost_estimate=pl.CostEstimate(
            flops=weight * count * rows * len(blocks) * rows * width,
            bytes_accessed=weight * rows * LANES,
            transcendentals=0,
        ),
    )(*queries, *sources, *state, *after, *carried)


def merge_kernel(p0, p1, p2, p3, x_ref, w_ref, hidden_ref, stats_ref):
    width = w_ref.shape[0]
    lane = lax.broadcasted_iota(jnp.int32, (LANES, width), 0)
    chan = lax.broadcasted_iota(jnp.int32, (LANES, width), 1)
    spread = jnp.zeros((LANES, width), F32)
    for piece in range(3):
        head = lane - 10 * piece
        inside = (head >= 0) & (head < 10) & (chan >= head * HEAD) & (chan < head * HEAD + HEAD)
        spread = jnp.where(inside, 1.0, spread)
    spread = spread.astype(BF)
    parts = (p0, p1, p2, p3)
    levels = [jnp.dot(p[:, width : width + LANES], spread, preferred_element_type=F32) for p in parts]
    top = functools.reduce(jnp.maximum, levels)
    shares = [jnp.exp(level - top) for level in levels]
    total = functools.reduce(jnp.add, shares)
    summed = functools.reduce(
        jnp.add, [s * p[:, :width].astype(F32) for s, p in zip(shares, parts)]
    )
    attended = (summed / total).astype(BF)
    hidden = x_ref[...].astype(F32) + jnp.dot(attended, w_ref[...], preferred_element_type=F32)
    hidden_ref[...] = hidden
    stats_ref[...] = local_stats(hidden, stats_ref.shape[0])


def merge(parts, x, w_out, peers):
    rows, channels = x.shape
    return pl.pallas_call(
        merge_kernel,
        out_shape=[
            jax.ShapeDtypeStruct((rows, channels), F32),
            jax.ShapeDtypeStruct((peers, LANES), F32),
        ],
        name="merge_project",
        compiler_params=pltpu.CompilerParams(vmem_limit_bytes=24 * 2**20),
        cost_estimate=pl.CostEstimate(
            flops=2 * rows * w_out.size, bytes_accessed=2 * w_out.size, transcendentals=0
        ),
    )(*parts, x, w_out)


def conv_kernel(stats_ref, hidden_ref, above_ref, below_ref, gain_ref, w_ref, shift_ref, out_ref, moved):
    own = lax.axis_index("patch")
    last = lax.axis_size("patch") - 1
    rows, channels = hidden_ref.shape
    cols = above_ref.shape[0]
    width = out_ref.shape[1]
    center, scale = combined(stats_ref[...], channels, rows * (channels // GROUPS))
    gain = gain_ref[...].reshape(1, channels)
    col = lax.broadcasted_iota(jnp.int32, (cols, channels), 0)
    pieces = [(above_ref, 0, own != 0)]
    pieces += [(hidden_ref, i, None) for i in range(rows // cols)]
    pieces += [(below_ref, 0, own != last)]
    for place, (ref, part, kept) in enumerate(pieces):
        v = (ref[part * cols : (part + 1) * cols, :] - center) * scale * gain
        v = v / (1.0 + jnp.exp(-v))
        if kept is not None:
            v = jnp.where(kept, v, 0.0)
        to = slice(place * cols, (place + 1) * cols)
        left = jnp.where(col == 0, 0.0, pltpu.roll(v, 1, 0))
        right = jnp.where(col == cols - 1, 0.0, pltpu.roll(v, cols - 1, 0))
        for tap, value in enumerate((left, v, right)):
            moved[to, tap * channels : (tap + 1) * channels] = value.astype(BF)
    total = hidden_ref[:, :width] + shift_ref[...].reshape(1, width)
    for tap in range(3):
        window = moved[tap * cols : tap * cols + rows, :]
        taps = w_ref[3 * tap : 3 * tap + 3].reshape(3 * channels, width)
        total = total + jnp.dot(window, taps, preferred_element_type=F32)
    out_ref[...] = total.astype(BF)


def convolve(stats, hidden, above, below, gain, weight, shift):
    rows, channels = hidden.shape
    cols = above.shape[0]
    width = weight.shape[2]
    return pl.pallas_call(
        conv_kernel,
        in_specs=[VMEM] * 7,
        out_specs=VMEM,
        out_shape=jax.ShapeDtypeStruct((rows, width), BF),
        scratch_shapes=[pltpu.VMEM((rows + 2 * cols, 3 * channels), BF)],
        name="norm_convolve",
        compiler_params=pltpu.CompilerParams(vmem_limit_bytes=24 * 2**20),
        cost_estimate=pl.CostEstimate(
            flops=2 * rows * weight.size, bytes_accessed=2 * weight.size, transcendentals=0
        ),
    )(stats, hidden, above, below, gain, weight, shift)


def everyones(stats):
    return lax.all_to_all(stats, "patch", 0, 0, tiled=True)


def shards(
    latent,
    gn_gain,
    w_query,
    w_key,
    w_value,
    w_out,
    stale_keys,
    stale_values,
    gn2_gain,
    conv_weight,
    time_shift,
):
    row_count, col_count, channels = latent.shape
    tok_count = row_count * col_count
    peers = lax.axis_size("patch")
    x = latent.reshape(tok_count, channels)
    stats, old, *weights = norm_stats(x, stale_keys, stale_values, (w_query, w_key, w_value), peers)
    from_below = shifted(old, 1, 0, 0)
    from_above = shifted(old, -1, 0, 0)
    from_side = shifted(old, 0, 0, 1)
    stats = everyones(stats)
    queries, fresh_keys, fresh_values, fresh = project(stats, x, gn_gain, *weights)

    relayed, _ = lax.optimization_barrier((from_side, stats))
    side_below = shifted(relayed, 1, 0, 0)
    side_above = shifted(relayed, -1, 0, 0)
    beside = [shifted(queries, 0, 1, 0), shifted(queries, 0, -1, 0)]
    across = [shifted(queries, 0, 2, 0)]
    last_keys = shifted(jnp.concatenate([from_below[:tok_count], side_below[:tok_count]]), 1, 0, 0)
    last_values = shifted(jnp.concatenate([from_above[tok_count:], side_above[tok_count:]]), -1, 0, 0)

    whole = lambda block: (block, 0, block, 1)
    near = [whole(from_below), whole(from_above), whole(from_side)]
    far = [whole(side_below), whole(side_above)]
    far += [(last_keys, 0, last_values, 0), (last_keys, 1, last_values, 1)]
    own_state = attend("near_own", [queries], [whole(fresh)] + near)
    beside_state = attend("near_beside", beside, [whole(old)] + near, after=own_state[1:2])
    across_state = attend("near_across", across, [whole(old)] + near, after=beside_state[1:2])
    (to_across,) = attend("far_across", across, far, across_state, final=True, extra=2)
    from_across = shifted(to_across, 0, 2, 0)
    to_beside = attend("far_beside", beside, far, beside_state, final=True, after=(to_across,), weight=1)
    own_part, weight = attend(
        "far_own", [queries], far, own_state, final=True, after=to_beside[:1], carry=conv_weight, weight=1
    )
    parts = (
        from_across,
        shifted(to_beside[0], 0, -1, 0),
        shifted(to_beside[1], 0, 1, 0),
        own_part,
    )
    hidden, stats = merge(parts, x, w_out, peers)
    down = [(i, i + 1) for i in range(peers - 1)]
    above = lax.ppermute(hidden[tok_count - col_count :], "patch", down)
    below = lax.ppermute(hidden[:col_count], "patch", [(j, i) for i, j in down])
    result = convolve(everyones(stats), hidden, above, below, gn2_gain, weight, time_shift)
    return (result.reshape(row_count, col_count, -1), fresh_keys, fresh_values)


def solution(mesh):
    placed = (
        P(("batch", "patch"), None, None),
        P(),
        P(),
        P(),
        P(),
        P(),
        P(("batch", "patch"), None),
        P(("batch", "patch"), None),
        P(),
        P(),
        P("batch"),
    )
    return jax.shard_map(
        shards,
        mesh=mesh,
        in_specs=placed,
        out_specs=(
            P(("batch", "patch"), None, None),
            P(("batch", "patch"), None),
            P(("batch", "patch"), None),
        ),
        check_vma=False,
    )
```

```python
import functools

import jax
import jax.numpy as jnp
from jax import lax
from jax.experimental import pallas as pl
from jax.experimental.pallas import tpu as pltpu
from jax.sharding import PartitionSpec as P

HEAD = 64
GROUPS = 32
LANES = 128
NY, NZ, NX = 4, 4, 2
EPS = 1e-05
BF = jnp.bfloat16
F32 = jnp.float32


def shifted(x, dy, dz, dx):
    pairs = []
    for y in range(NY):
        for z in range(NZ):
            for c in range(NX):
                to = (((y + dy) % NY) * NZ + (z + dz) % NZ) * NX + (c + dx) % NX
                pairs.append(((y * NZ + z) * NX + c, to))
    return lax.ppermute(x, "patch", pairs)


def members_of(channels, lead, offset):
    width = channels // GROUPS
    shape = (channels, LANES) if lead else (LANES, channels)
    chan = lax.broadcasted_iota(jnp.int32, shape, 0 if lead else 1)
    group = lax.broadcasted_iota(jnp.int32, shape, 1 if lead else 0) - offset
    inside = (chan >= group * width) & (chan < group * width + width)
    return jnp.where(inside, 1.0, 0.0).astype(BF)


def exact_dot(row, ones):
    at = lax.broadcasted_iota(jnp.int32, (16, row.shape[1]), 0)
    rest, cut = row, jnp.zeros((16, row.shape[1]), F32)
    for piece in range(3):
        part = rest.astype(BF).astype(F32)
        rest = rest - part
        cut = jnp.where(at == piece, part, cut)
    return jnp.sum(
        jnp.dot(cut.astype(BF), ones, preferred_element_type=F32), axis=0, keepdims=True
    )


def local_stats(x, peers):
    rows, channels = x.shape
    count = rows * (channels // GROUPS)
    total = jnp.sum(x, axis=0, keepdims=True)
    mean = exact_dot(total, members_of(channels, True, 0)) / count
    center = exact_dot(mean, members_of(channels, False, 0))
    squares = jnp.sum(jnp.square(x - center), axis=0, keepdims=True)
    spread = exact_dot(squares, members_of(channels, True, GROUPS))
    return jnp.broadcast_to(mean + spread, (peers, LANES))


def combined(stats, channels, count):
    peers = stats.shape[0]
    total = jnp.sum(stats, axis=0, keepdims=True)
    mean = total / peers
    between = jnp.sum(jnp.square(stats - mean), axis=0, keepdims=True) * count
    lead = members_of(channels, False, 0)
    center = exact_dot(mean, lead)
    spread = exact_dot(between, lead) + exact_dot(total, members_of(channels, False, GROUPS))
    return center, lax.rsqrt(spread / (count * peers) + EPS)


def full(shape):
    return pl.BlockSpec(shape, lambda *_: (0,) * len(shape))


HBM = pl.BlockSpec(memory_space=pltpu.HBM)
VMEM = pl.BlockSpec(memory_space=pltpu.VMEM)


def halves(src, dst, sems, first):
    size = src.shape[0] // 2
    return [
        pltpu.make_async_copy(
            src.at[i * size : (i + 1) * size], dst.at[i * size : (i + 1) * size], sems.at[first + i]
        )
        for i in range(2)
    ]


def stats_kernel(x_ref, k_ref, v_ref, wq, wk, wv, out_ref, old_ref, wq_out, wk_out, wv_out, held, sems):
    rows = k_ref.shape[0]
    copies = halves(x_ref, held, sems, 0)
    copies.append(pltpu.make_async_copy(k_ref, old_ref.at[0:rows], sems.at[2]))
    copies.append(pltpu.make_async_copy(v_ref, old_ref.at[rows : 2 * rows], sems.at[3]))
    for i, (src, dst) in enumerate(((wq, wq_out), (wk, wk_out), (wv, wv_out))):
        copies += halves(src, dst, sems, 4 + 2 * i)
    for copy in copies:
        copy.start()
    for copy in copies[:2]:
        copy.wait()
    out_ref[...] = local_stats(held[...].astype(F32), out_ref.shape[0])
    for copy in copies[2:]:
        copy.wait()


def norm_stats(x, keys, values, weights, peers):
    rows, width = keys.shape
    return pl.pallas_call(
        stats_kernel,
        in_specs=[HBM] * 6,
        out_specs=[VMEM] * 5,
        out_shape=[
            jax.ShapeDtypeStruct((peers, LANES), F32),
            jax.ShapeDtypeStruct((2 * rows, width), BF),
        ]
        + [pltpu.VMEM(w.shape, w.dtype) for w in weights],
        scratch_shapes=[pltpu.VMEM(x.shape, x.dtype), pltpu.SemaphoreType.DMA((10,))],
        name="norm_stats",
        compiler_params=pltpu.CompilerParams(vmem_limit_bytes=60030976),
        cost_estimate=pl.CostEstimate(flops=4 * x.size, bytes_accessed=2 * x.size, transcendentals=0),
    )(x, keys, values, *weights)


def project_kernel(stats_ref, x_ref, gain_ref, wq, wk, wv, q_ref, k_ref, v_ref, both_ref):
    rows, channels = x_ref.shape
    center, scale = combined(stats_ref[...], channels, rows * (channels // GROUPS))
    gain = gain_ref[...].reshape(1, channels)
    normed = ((x_ref[...].astype(F32) - center) * scale * gain).astype(BF)
    for i, (w_ref, o_ref) in enumerate(((wq, q_ref), (wk, k_ref), (wv, v_ref))):
        found = jnp.dot(normed, w_ref[...], preferred_element_type=F32).astype(BF)
        o_ref[...] = found
        if i > 0:
            both_ref[(i - 1) * rows : i * rows, :] = found


def project(stats, x, gain, wq, wk, wv):
    rows, channels = x.shape
    width = wq.shape[1]
    return pl.pallas_call(
        project_kernel,
        in_specs=[VMEM] * 6,
        out_specs=[VMEM] * 4,
        out_shape=[jax.ShapeDtypeStruct((rows, width), BF)] * 3
        + [jax.ShapeDtypeStruct((2 * rows, width), BF)],
        name="project",
        compiler_params=pltpu.CompilerParams(vmem_limit_bytes=24 * 2**20),
        cost_estimate=pl.CostEstimate(
            flops=6 * rows * channels * width,
            bytes_accessed=6 * channels * width,
            transcendentals=0,
        ),
    )(stats, x, gain, wq, wk, wv)


def attend_pair(queries, keys, values):
    rows = queries.shape[0]
    first = lax.broadcasted_iota(jnp.int32, (rows, LANES), 1) < HEAD
    scaled = queries * BF(0.125)
    none = jnp.zeros_like(scaled)
    found = []
    for mine in (jnp.where(first, scaled, none), jnp.where(first, none, scaled)):
        scores = lax.dot_general(
            mine, keys, (((1,), (1,)), ((), ())), preferred_element_type=F32
        )
        top = jnp.max(scores, axis=1, keepdims=True)
        weights = jnp.exp(scores - top).astype(BF)
        both = jnp.dot(weights, values, preferred_element_type=F32)
        found.append((both[:, :LANES], jnp.broadcast_to(top, (rows, LANES)), both[:, LANES:]))
    return first, found


def attend_kernel(plan, start, final, waits, carry, unroll, *refs):
    count, rows_of = plan
    refs = list(refs)
    take = lambda n: [refs.pop(0) for _ in range(n)]
    queries, sources = take(count), take(2 * len(rows_of))
    state = take(3) if start else None
    take(waits)
    brought = take(1 if carry else 0)
    outs = take(count if final else 3)
    copies = []
    if carry:
        (kept,), (sems,) = take(1), take(1)
        copies = [
            pltpu.make_async_copy(brought[0].at[i], kept.at[i], sems.at[i]) for i in range(kept.shape[0])
        ]
        for copy in copies:
            copy.start()
    rows, width = queries[0].shape
    lane = lax.broadcasted_iota(jnp.int32, (rows, LANES), 1)
    ones = jnp.ones((rows, LANES), BF)
    if final:
        for o_ref in outs:
            o_ref[:, width:] = jnp.zeros((rows, o_ref.shape[1] - width), BF)

    def pair(j, carried):
        cols = pl.ds(pl.multiple_of(j * LANES, LANES), LANES)
        keys, values = [], []
        for i, (key_row, value_row) in enumerate(rows_of):
            keys.append(sources[2 * i][key_row * rows : (key_row + 1) * rows, cols])
            value = sources[2 * i + 1][value_row * rows : (value_row + 1) * rows, cols]
            values.append(jnp.concatenate([value, ones], axis=1))
        keys, values = jnp.concatenate(keys, axis=0), jnp.concatenate(values, axis=0)
        for band, q_ref in enumerate(queries):
            first, found = attend_pair(q_ref[:, cols], keys, values)
            at = slice(band * rows, (band + 1) * rows)
            summed, top, total = (jnp.where(first, found[0][n], found[1][n]) for n in range(3))
            if state is not None:
                old_top = state[1][at, cols]
                new_top = jnp.maximum(top, old_top)
                part, old_part = jnp.exp(top - new_top), jnp.exp(old_top - new_top)
                top = new_top
                total = part * total + old_part * state[2][at, cols]
                summed = part * summed + old_part * state[0][at, cols]
            if not final:
                for out_ref, value in zip(outs, (summed, top, total)):
                    out_ref[at, cols] = value
                continue
            outs[band][:, cols] = (summed / total).astype(BF)
            level = top + jnp.log(total)
            swapped = pltpu.roll(level, HEAD, 1)
            row_level = (jnp.where(first, level, swapped), jnp.where(first, swapped, level))
            extra = outs[band][:, width : width + LANES]
            for h in range(2):
                rest = row_level[h]
                for piece in range(3):
                    part = rest.astype(BF)
                    rest = rest - part.astype(F32)
                    extra = jnp.where(lane == 2 * j + h + 10 * piece, part, extra)
            outs[band][:, width : width + LANES] = extra
        return carried

    lax.fori_loop(0, width // LANES, pair, 0, unroll=unroll)
    for copy in copies:
        copy.wait()


def attend(name, queries, blocks, state=None, final=False, after=(), carry=None, weight=16, extra=1, unroll=False):
    rows, width = queries[0].shape
    count = len(queries)
    sources = []
    for keys, _, values, _ in blocks:
        sources += [keys, values]
    plan = (count, [(key_row, value_row) for _, key_row, _, value_row in blocks])
    if final:
        out_shape = [jax.ShapeDtypeStruct((rows, width + extra * LANES), BF)] * count
    else:
        out_shape = [jax.ShapeDtypeStruct((count * rows, width), F32)] * 3
    scratch, carried = [], []
    if carry is not None:
        out_shape.append(pltpu.VMEM(carry.shape, carry.dtype))
        scratch.append(pltpu.SemaphoreType.DMA((carry.shape[0],)))
        carried.append(carry)
    state = tuple(state or ())
    return pl.pallas_call(
        functools.partial(attend_kernel, plan, bool(state), final, len(after), carry is not None, unroll),
        in_specs=[VMEM] * (count + len(sources) + len(state))
        + [pl.BlockSpec(memory_space=pl.ANY)] * len(after)
        + [HBM] * len(carried),
        out_specs=[VMEM] * len(out_shape),
        out_shape=out_shape,
        scratch_shapes=scratch,
        name=name,
        compiler_params=pltpu.CompilerParams(vmem_limit_bytes=24 * 2**20),
        cost_estimate=pl.CostEstimate(
            flops=weight * count * rows * len(blocks) * rows * width,
            bytes_accessed=weight * rows * LANES,
            transcendentals=0,
        ),
    )(*queries, *sources, *state, *after, *carried)


def merge_kernel(p0, p1, p2, p3, x_ref, w_ref, hidden_ref, stats_ref):
    width = w_ref.shape[0]
    lane = lax.broadcasted_iota(jnp.int32, (LANES, width), 0)
    chan = lax.broadcasted_iota(jnp.int32, (LANES, width), 1)
    spread = jnp.zeros((LANES, width), F32)
    for piece in range(3):
        head = lane - 10 * piece
        inside = (head >= 0) & (head < 10) & (chan >= head * HEAD) & (chan < head * HEAD + HEAD)
        spread = jnp.where(inside, 1.0, spread)
    spread = spread.astype(BF)
    parts = (p0, p1, p2, p3)
    levels = [jnp.dot(p[:, width : width + LANES], spread, preferred_element_type=F32) for p in parts]
    top = functools.reduce(jnp.maximum, levels)
    shares = [jnp.exp(level - top) for level in levels]
    total = functools.reduce(jnp.add, shares)
    summed = functools.reduce(
        jnp.add, [s * p[:, :width].astype(F32) for s, p in zip(shares, parts)]
    )
    attended = (summed / total).astype(BF)
    hidden = x_ref[...].astype(F32) + jnp.dot(attended, w_ref[...], preferred_element_type=F32)
    hidden_ref[...] = hidden
    stats_ref[...] = local_stats(hidden, stats_ref.shape[0])


def merge(parts, x, w_out, peers):
    rows, channels = x.shape
    return pl.pallas_call(
        merge_kernel,
        out_shape=[
            jax.ShapeDtypeStruct((rows, channels), F32),
            jax.ShapeDtypeStruct((peers, LANES), F32),
        ],
        name="merge_project",
        compiler_params=pltpu.CompilerParams(vmem_limit_bytes=24 * 2**20),
        cost_estimate=pl.CostEstimate(
            flops=2 * rows * w_out.size, bytes_accessed=2 * w_out.size, transcendentals=0
        ),
    )(*parts, x, w_out)


def conv_kernel(stats_ref, hidden_ref, above_ref, below_ref, gain_ref, w_ref, shift_ref, out_ref, moved):
    own = lax.axis_index("patch")
    last = lax.axis_size("patch") - 1
    rows, channels = hidden_ref.shape
    cols = above_ref.shape[0]
    width = out_ref.shape[1]
    center, scale = combined(stats_ref[...], channels, rows * (channels // GROUPS))
    gain = gain_ref[...].reshape(1, channels)
    col = lax.broadcasted_iota(jnp.int32, (cols, channels), 0)
    pieces = [(above_ref, 0, own != 0)]
    pieces += [(hidden_ref, i, None) for i in range(rows // cols)]
    pieces += [(below_ref, 0, own != last)]
    for place, (ref, part, kept) in enumerate(pieces):
        v = (ref[part * cols : (part + 1) * cols, :] - center) * scale * gain
        v = v / (1.0 + jnp.exp(-v))
        if kept is not None:
            v = jnp.where(kept, v, 0.0)
        to = slice(place * cols, (place + 1) * cols)
        left = jnp.where(col == 0, 0.0, pltpu.roll(v, 1, 0))
        right = jnp.where(col == cols - 1, 0.0, pltpu.roll(v, cols - 1, 0))
        for tap, value in enumerate((left, v, right)):
            moved[to, tap * channels : (tap + 1) * channels] = value.astype(BF)
    total = hidden_ref[:, :width] + shift_ref[...].reshape(1, width)
    for tap in range(3):
        window = moved[tap * cols : tap * cols + rows, :]
        taps = w_ref[3 * tap : 3 * tap + 3].reshape(3 * channels, width)
        total = total + jnp.dot(window, taps, preferred_element_type=F32)
    out_ref[...] = total.astype(BF)


def convolve(stats, hidden, above, below, gain, weight, shift):
    rows, channels = hidden.shape
    cols = above.shape[0]
    width = weight.shape[2]
    return pl.pallas_call(
        conv_kernel,
        in_specs=[VMEM] * 7,
        out_specs=VMEM,
        out_shape=jax.ShapeDtypeStruct((rows, width), BF),
        scratch_shapes=[pltpu.VMEM((rows + 2 * cols, 3 * channels), BF)],
        name="norm_convolve",
        compiler_params=pltpu.CompilerParams(vmem_limit_bytes=24 * 2**20),
        cost_estimate=pl.CostEstimate(
            flops=2 * rows * weight.size, bytes_accessed=2 * weight.size, transcendentals=0
        ),
    )(stats, hidden, above, below, gain, weight, shift)


def everyones(stats):
    return lax.all_to_all(stats, "patch", 0, 0, tiled=True)


def shards(
    latent,
    gn_gain,
    w_query,
    w_key,
    w_value,
    w_out,
    stale_keys,
    stale_values,
    gn2_gain,
    conv_weight,
    time_shift,
):
    row_count, col_count, channels = latent.shape
    tok_count = row_count * col_count
    peers = lax.axis_size("patch")
    x = latent.reshape(tok_count, channels)
    stats, old, *weights = norm_stats(x, stale_keys, stale_values, (w_query, w_key, w_value), peers)
    from_below = shifted(old, 1, 0, 0)
    from_above = shifted(old, -1, 0, 0)
    from_side = shifted(old, 0, 0, 1)
    stats = everyones(stats)
    queries, fresh_keys, fresh_values, fresh = project(stats, x, gn_gain, *weights)

    relayed, _ = lax.optimization_barrier((from_side, stats))
    side_below = shifted(relayed, 1, 0, 0)
    side_above = shifted(relayed, -1, 0, 0)
    beside = [shifted(queries, 0, 1, 0), shifted(queries, 0, -1, 0)]
    across = [shifted(queries, 0, 2, 0)]
    last_keys = shifted(jnp.concatenate([from_below[:tok_count], side_below[:tok_count]]), 1, 0, 0)
    last_values = shifted(jnp.concatenate([from_above[tok_count:], side_above[tok_count:]]), -1, 0, 0)

    whole = lambda block: (block, 0, block, 1)
    near = [whole(from_below), whole(from_above), whole(from_side)]
    far = [whole(side_below), whole(side_above)]
    far += [(last_keys, 0, last_values, 0), (last_keys, 1, last_values, 1)]
    own_state = attend("near_own", [queries], [whole(fresh)] + near)
    beside_state = attend("near_beside", beside, [whole(old)] + near, after=own_state[1:2], unroll=True)
    across_state = attend("near_across", across, [whole(old)] + near, after=beside_state[1:2])
    (to_across,) = attend("far_across", across, far, across_state, final=True, extra=2)
    from_across = shifted(to_across, 0, 2, 0)
    to_beside = attend("far_beside", beside, far, beside_state, final=True, after=(to_across,), weight=1, unroll=True)
    own_part, weight = attend(
        "far_own", [queries], far, own_state, final=True, after=to_beside[:1], carry=conv_weight, weight=1
    )
    parts = (
        from_across,
        shifted(to_beside[0], 0, -1, 0),
        shifted(to_beside[1], 0, 1, 0),
        own_part,
    )
    hidden, stats = merge(parts, x, w_out, peers)
    down = [(i, i + 1) for i in range(peers - 1)]
    above = lax.ppermute(hidden[tok_count - col_count :], "patch", down)
    below = lax.ppermute(hidden[:col_count], "patch", [(j, i) for i, j in down])
    result = convolve(everyones(stats), hidden, above, below, gn2_gain, weight, time_shift)
    return (result.reshape(row_count, col_count, -1), fresh_keys, fresh_values)


def solution(mesh):
    placed = (
        P(("batch", "patch"), None, None),
        P(),
        P(),
        P(),
        P(),
        P(),
        P(("batch", "patch"), None),
        P(("batch", "patch"), None),
        P(),
        P(),
        P("batch"),
    )
    return jax.shard_map(
        shards,
        mesh=mesh,
        in_specs=placed,
        out_specs=(
            P(("batch", "patch"), None, None),
            P(("batch", "patch"), None),
            P(("batch", "patch"), None),
        ),
        check_vma=False,
    )
```

```python
import functools

import jax
import jax.numpy as jnp
from jax import lax
from jax.experimental import pallas as pl
from jax.experimental.pallas import tpu as pltpu
from jax.sharding import PartitionSpec as P

HEAD = 64
GROUPS = 32
LANES = 128
NY, NZ, NX = 4, 4, 2
EPS = 1e-05
BF = jnp.bfloat16
F32 = jnp.float32


def shifted(x, dy, dz, dx):
    pairs = []
    for y in range(NY):
        for z in range(NZ):
            for c in range(NX):
                to = (((y + dy) % NY) * NZ + (z + dz) % NZ) * NX + (c + dx) % NX
                pairs.append(((y * NZ + z) * NX + c, to))
    return lax.ppermute(x, "patch", pairs)


def members_of(channels, lead, offset):
    width = channels // GROUPS
    shape = (channels, LANES) if lead else (LANES, channels)
    chan = lax.broadcasted_iota(jnp.int32, shape, 0 if lead else 1)
    group = lax.broadcasted_iota(jnp.int32, shape, 1 if lead else 0) - offset
    inside = (chan >= group * width) & (chan < group * width + width)
    return jnp.where(inside, 1.0, 0.0).astype(BF)


def exact_dot(row, ones):
    at = lax.broadcasted_iota(jnp.int32, (16, row.shape[1]), 0)
    rest, cut = row, jnp.zeros((16, row.shape[1]), F32)
    for piece in range(3):
        part = rest.astype(BF).astype(F32)
        rest = rest - part
        cut = jnp.where(at == piece, part, cut)
    return jnp.sum(
        jnp.dot(cut.astype(BF), ones, preferred_element_type=F32), axis=0, keepdims=True
    )


def group_matrices(channels):
    return (
        members_of(channels, True, 0),
        members_of(channels, False, 0),
        members_of(channels, True, GROUPS),
    )


def local_stats(x, peers, matrices):
    rows, channels = x.shape
    count = rows * (channels // GROUPS)
    total = jnp.sum(x, axis=0, keepdims=True)
    mean = exact_dot(total, matrices[0]) / count
    center = exact_dot(mean, matrices[1])
    squares = jnp.sum(jnp.square(x - center), axis=0, keepdims=True)
    spread = exact_dot(squares, matrices[2])
    return jnp.broadcast_to(mean + spread, (peers, LANES))


def combined(stats, channels, count):
    peers = stats.shape[0]
    total = jnp.sum(stats, axis=0, keepdims=True)
    mean = total / peers
    between = jnp.sum(jnp.square(stats - mean), axis=0, keepdims=True) * count
    lead = members_of(channels, False, 0)
    center = exact_dot(mean, lead)
    spread = exact_dot(between, lead) + exact_dot(total, members_of(channels, False, GROUPS))
    return center, lax.rsqrt(spread / (count * peers) + EPS)


def full(shape):
    return pl.BlockSpec(shape, lambda *_: (0,) * len(shape))


HBM = pl.BlockSpec(memory_space=pltpu.HBM)
VMEM = pl.BlockSpec(memory_space=pltpu.VMEM)


def halves(src, dst, sems, first):
    size = src.shape[0] // 2
    return [
        pltpu.make_async_copy(
            src.at[i * size : (i + 1) * size], dst.at[i * size : (i + 1) * size], sems.at[first + i]
        )
        for i in range(2)
    ]


def stats_kernel(x_ref, k_ref, v_ref, wq, wk, wv, out_ref, old_ref, wq_out, wk_out, wv_out, held, sems):
    rows = k_ref.shape[0]
    copies = halves(x_ref, held, sems, 0)
    copies.append(pltpu.make_async_copy(k_ref, old_ref.at[0:rows], sems.at[2]))
    copies.append(pltpu.make_async_copy(v_ref, old_ref.at[rows : 2 * rows], sems.at[3]))
    for i, (src, dst) in enumerate(((wq, wq_out), (wk, wk_out), (wv, wv_out))):
        copies += halves(src, dst, sems, 4 + 2 * i)
    for copy in copies:
        copy.start()
    matrices = group_matrices(x_ref.shape[1])
    for copy in copies[:2]:
        copy.wait()
    out_ref[...] = local_stats(held[...].astype(F32), out_ref.shape[0], matrices)
    for copy in copies[2:]:
        copy.wait()


def norm_stats(x, keys, values, weights, peers):
    rows, width = keys.shape
    return pl.pallas_call(
        stats_kernel,
        in_specs=[HBM] * 6,
        out_specs=[VMEM] * 5,
        out_shape=[
            jax.ShapeDtypeStruct((peers, LANES), F32),
            jax.ShapeDtypeStruct((2 * rows, width), BF),
        ]
        + [pltpu.VMEM(w.shape, w.dtype) for w in weights],
        scratch_shapes=[pltpu.VMEM(x.shape, x.dtype), pltpu.SemaphoreType.DMA((10,))],
        name="norm_stats",
        compiler_params=pltpu.CompilerParams(vmem_limit_bytes=60030976),
        cost_estimate=pl.CostEstimate(flops=4 * x.size, bytes_accessed=2 * x.size, transcendentals=0),
    )(x, keys, values, *weights)


def project_kernel(stats_ref, x_ref, gain_ref, wq, wk, wv, q_ref, k_ref, v_ref, both_ref):
    rows, channels = x_ref.shape
    center, scale = combined(stats_ref[...], channels, rows * (channels // GROUPS))
    gain = gain_ref[...].reshape(1, channels)
    normed = ((x_ref[...].astype(F32) - center) * scale * gain).astype(BF)
    for i, (w_ref, o_ref) in enumerate(((wq, q_ref), (wk, k_ref), (wv, v_ref))):
        found = jnp.dot(normed, w_ref[...], preferred_element_type=F32).astype(BF)
        o_ref[...] = found
        if i > 0:
            both_ref[(i - 1) * rows : i * rows, :] = found


def project(stats, x, gain, wq, wk, wv):
    rows, channels = x.shape
    width = wq.shape[1]
    return pl.pallas_call(
        project_kernel,
        in_specs=[VMEM] * 6,
        out_specs=[VMEM] * 4,
        out_shape=[jax.ShapeDtypeStruct((rows, width), BF)] * 3
        + [jax.ShapeDtypeStruct((2 * rows, width), BF)],
        name="project",
        compiler_params=pltpu.CompilerParams(vmem_limit_bytes=24 * 2**20),
        cost_estimate=pl.CostEstimate(
            flops=6 * rows * channels * width,
            bytes_accessed=6 * channels * width,
            transcendentals=0,
        ),
    )(stats, x, gain, wq, wk, wv)


def scores_of(queries, keys, second):
    lane = lax.broadcasted_iota(jnp.int32, queries.shape, 1)
    mine = jnp.where((lane >= HEAD) if second else (lane < HEAD), queries * BF(0.125), BF(0))
    return lax.dot_general(mine, keys, (((1,), (1,)), ((), ())), preferred_element_type=F32)


def weigh(scores, values):
    top = jnp.max(scores, axis=1, keepdims=True)
    weights = jnp.exp(scores - top).astype(BF)
    both = jnp.dot(weights, values, preferred_element_type=F32)
    return both[:, :LANES], jnp.broadcast_to(top, (scores.shape[0], LANES)), both[:, LANES:]


def attend_kernel(plan, start, final, waits, carry, unroll, *refs):
    count, rows_of = plan
    refs = list(refs)
    take = lambda n: [refs.pop(0) for _ in range(n)]
    queries, sources = take(count), take(2 * len(rows_of))
    state = take(3) if start else None
    take(waits)
    brought = take(1 if carry else 0)
    outs = take(count if final else 3)
    copies = []
    (kept,) = take(1) if carry else (None,)
    (scores,) = take(1)
    if carry:
        (sems,) = take(1)
        copies = [
            pltpu.make_async_copy(brought[0].at[i], kept.at[i], sems.at[i]) for i in range(kept.shape[0])
        ]
        for copy in copies:
            copy.start()
    rows, width = queries[0].shape
    lane = lax.broadcasted_iota(jnp.int32, (rows, LANES), 1)
    ones = jnp.ones((rows, LANES), BF)
    if final:
        for o_ref in outs:
            o_ref[:, width:] = jnp.zeros((rows, o_ref.shape[1] - width), BF)

    pairs = width // LANES
    lanes_of = lambda j: pl.ds(pl.multiple_of(j * LANES, LANES), LANES)
    piece = lambda ref, row, cols: ref[row * rows : (row + 1) * rows, cols]

    def keys_of(cols):
        return jnp.concatenate([piece(sources[2 * i], r, cols) for i, (r, _) in enumerate(rows_of)])

    def values_of(cols):
        found = [piece(sources[2 * i + 1], r, cols) for i, (_, r) in enumerate(rows_of)]
        return jnp.concatenate([jnp.concatenate([v, ones], axis=1) for v in found])

    def step(j, following):
        cols = lanes_of(j)
        values = values_of(cols)
        if following:
            later = lanes_of(j + 1)
            keys = keys_of(later)
        for band, q_ref in enumerate(queries):
            found = []
            for h in range(2):
                found.append(weigh(scores[2 * band + h], values))
                if following:
                    scores[2 * band + h] = scores_of(q_ref[:, later], keys, h)
            first = lane < HEAD
            at = slice(band * rows, (band + 1) * rows)
            summed, top, total = (jnp.where(first, found[0][n], found[1][n]) for n in range(3))
            if state is not None:
                old_top = state[1][at, cols]
                new_top = jnp.maximum(top, old_top)
                part, old_part = jnp.exp(top - new_top), jnp.exp(old_top - new_top)
                top = new_top
                total = part * total + old_part * state[2][at, cols]
                summed = part * summed + old_part * state[0][at, cols]
            if not final:
                for out_ref, value in zip(outs, (summed, top, total)):
                    out_ref[at, cols] = value
                continue
            outs[band][:, cols] = (summed / total).astype(BF)
            level = top + jnp.log(total)
            swapped = pltpu.roll(level, HEAD, 1)
            row_level = (jnp.where(first, level, swapped), jnp.where(first, swapped, level))
            extra = outs[band][:, width : width + LANES]
            for h in range(2):
                rest = row_level[h]
                for cut in range(3):
                    part = rest.astype(BF)
                    rest = rest - part.astype(F32)
                    extra = jnp.where(lane == 2 * j + h + 10 * cut, part, extra)
            outs[band][:, width : width + LANES] = extra

    start_keys = keys_of(slice(0, LANES))
    for band, q_ref in enumerate(queries):
        for h in range(2):
            scores[2 * band + h] = scores_of(q_ref[:, 0:LANES], start_keys, h)

    def loop_step(j, carried):
        step(j, True)
        return carried

    lax.fori_loop(0, pairs - 1, loop_step, 0, unroll=unroll)
    step(pairs - 1, False)
    for copy in copies:
        copy.wait()


def attend(name, queries, blocks, state=None, final=False, after=(), carry=None, weight=16, extra=1, unroll=False):
    rows, width = queries[0].shape
    count = len(queries)
    sources = []
    for keys, _, values, _ in blocks:
        sources += [keys, values]
    plan = (count, [(key_row, value_row) for _, key_row, _, value_row in blocks])
    if final:
        out_shape = [jax.ShapeDtypeStruct((rows, width + extra * LANES), BF)] * count
    else:
        out_shape = [jax.ShapeDtypeStruct((count * rows, width), F32)] * 3
    scratch = [pltpu.VMEM((2 * count, rows, len(blocks) * rows), F32)]
    carried = []
    if carry is not None:
        out_shape.append(pltpu.VMEM(carry.shape, carry.dtype))
        scratch.append(pltpu.SemaphoreType.DMA((carry.shape[0],)))
        carried.append(carry)
    state = tuple(state or ())
    return pl.pallas_call(
        functools.partial(attend_kernel, plan, bool(state), final, len(after), carry is not None, unroll),
        in_specs=[VMEM] * (count + len(sources) + len(state))
        + [pl.BlockSpec(memory_space=pl.ANY)] * len(after)
        + [HBM] * len(carried),
        out_specs=[VMEM] * len(out_shape),
        out_shape=out_shape,
        scratch_shapes=scratch,
        name=name,
        compiler_params=pltpu.CompilerParams(vmem_limit_bytes=24 * 2**20),
        cost_estimate=pl.CostEstimate(
            flops=weight * count * rows * len(blocks) * rows * width,
            bytes_accessed=weight * rows * LANES,
            transcendentals=0,
        ),
    )(*queries, *sources, *state, *after, *carried)


def merge_kernel(p0, p1, p2, p3, x_ref, w_ref, hidden_ref, stats_ref):
    width = w_ref.shape[0]
    lane = lax.broadcasted_iota(jnp.int32, (LANES, width), 0)
    chan = lax.broadcasted_iota(jnp.int32, (LANES, width), 1)
    spread = jnp.zeros((LANES, width), F32)
    for piece in range(3):
        head = lane - 10 * piece
        inside = (head >= 0) & (head < 10) & (chan >= head * HEAD) & (chan < head * HEAD + HEAD)
        spread = jnp.where(inside, 1.0, spread)
    spread = spread.astype(BF)
    parts = (p0, p1, p2, p3)
    levels = [jnp.dot(p[:, width : width + LANES], spread, preferred_element_type=F32) for p in parts]
    top = functools.reduce(jnp.maximum, levels)
    shares = [jnp.exp(level - top) for level in levels]
    total = functools.reduce(jnp.add, shares)
    summed = functools.reduce(
        jnp.add, [s * p[:, :width].astype(F32) for s, p in zip(shares, parts)]
    )
    attended = (summed / total).astype(BF)
    hidden = x_ref[...].astype(F32) + jnp.dot(attended, w_ref[...], preferred_element_type=F32)
    hidden_ref[...] = hidden
    stats_ref[...] = local_stats(hidden, stats_ref.shape[0], group_matrices(hidden.shape[1]))


def merge(parts, x, w_out, peers):
    rows, channels = x.shape
    return pl.pallas_call(
        merge_kernel,
        out_shape=[
            jax.ShapeDtypeStruct((rows, channels), F32),
            jax.ShapeDtypeStruct((peers, LANES), F32),
        ],
        name="merge_project",
        compiler_params=pltpu.CompilerParams(vmem_limit_bytes=24 * 2**20),
        cost_estimate=pl.CostEstimate(
            flops=2 * rows * w_out.size, bytes_accessed=2 * w_out.size, transcendentals=0
        ),
    )(*parts, x, w_out)


def conv_kernel(stats_ref, hidden_ref, above_ref, below_ref, gain_ref, w_ref, shift_ref, out_ref, moved):
    own = lax.axis_index("patch")
    last = lax.axis_size("patch") - 1
    rows, channels = hidden_ref.shape
    cols = above_ref.shape[0]
    width = out_ref.shape[1]
    center, scale = combined(stats_ref[...], channels, rows * (channels // GROUPS))
    scale = 0.5 * scale * gain_ref[...].reshape(1, channels)
    col = lax.broadcasted_iota(jnp.int32, (cols, channels), 0)
    pieces = [(above_ref, 0, own != 0)]
    pieces += [(hidden_ref, i, None) for i in range(rows // cols)]
    pieces += [(below_ref, 0, own != last)]
    for place, (ref, part, kept) in enumerate(pieces):
        half = (ref[part * cols : (part + 1) * cols, :] - center) * scale
        v = half * jnp.tanh(half) + half
        if kept is not None:
            v = jnp.where(kept, v, 0.0)
        to = slice(place * cols, (place + 1) * cols)
        left = jnp.where(col == 0, 0.0, pltpu.roll(v, 1, 0))
        right = jnp.where(col == cols - 1, 0.0, pltpu.roll(v, cols - 1, 0))
        for tap, value in enumerate((left, v, right)):
            moved[to, tap * channels : (tap + 1) * channels] = value.astype(BF)
    total = hidden_ref[:, :width] + shift_ref[...].reshape(1, width)
    for tap in range(3):
        window = moved[tap * cols : tap * cols + rows, :]
        taps = w_ref[3 * tap : 3 * tap + 3].reshape(3 * channels, width)
        total = total + jnp.dot(window, taps, preferred_element_type=F32)
    out_ref[...] = total.astype(BF)


def convolve(stats, hidden, above, below, gain, weight, shift):
    rows, channels = hidden.shape
    cols = above.shape[0]
    width = weight.shape[2]
    return pl.pallas_call(
        conv_kernel,
        in_specs=[VMEM] * 7,
        out_specs=VMEM,
        out_shape=jax.ShapeDtypeStruct((rows, width), BF),
        scratch_shapes=[pltpu.VMEM((rows + 2 * cols, 3 * channels), BF)],
        name="norm_convolve",
        compiler_params=pltpu.CompilerParams(vmem_limit_bytes=24 * 2**20),
        cost_estimate=pl.CostEstimate(
            flops=2 * rows * weight.size, bytes_accessed=2 * weight.size, transcendentals=0
        ),
    )(stats, hidden, above, below, gain, weight, shift)


def everyones(stats):
    return lax.all_to_all(stats, "patch", 0, 0, tiled=True)


def shards(
    latent,
    gn_gain,
    w_query,
    w_key,
    w_value,
    w_out,
    stale_keys,
    stale_values,
    gn2_gain,
    conv_weight,
    time_shift,
):
    row_count, col_count, channels = latent.shape
    tok_count = row_count * col_count
    peers = lax.axis_size("patch")
    x = latent.reshape(tok_count, channels)
    stats, old, *weights = norm_stats(x, stale_keys, stale_values, (w_query, w_key, w_value), peers)
    from_below = shifted(old, 1, 0, 0)
    from_above = shifted(old, -1, 0, 0)
    from_side = shifted(old, 0, 0, 1)
    stats = everyones(stats)
    queries, fresh_keys, fresh_values, fresh = project(stats, x, gn_gain, *weights)

    relayed, _ = lax.optimization_barrier((from_side, stats))
    side_below = shifted(relayed, 1, 0, 0)
    side_above = shifted(relayed, -1, 0, 0)
    beside = [shifted(queries, 0, 1, 0), shifted(queries, 0, -1, 0)]
    across = [shifted(queries, 0, 2, 0)]
    last_keys = shifted(jnp.concatenate([from_below[:tok_count], side_below[:tok_count]]), 1, 0, 0)
    last_values = shifted(jnp.concatenate([from_above[tok_count:], side_above[tok_count:]]), -1, 0, 0)

    whole = lambda block: (block, 0, block, 1)
    near = [whole(from_below), whole(from_above), whole(from_side)]
    far = [whole(side_below), whole(side_above)]
    far += [(last_keys, 0, last_values, 0), (last_keys, 1, last_values, 1)]
    own_state = attend("near_own", [queries], [whole(fresh)] + near)
    beside_state = attend("near_beside", beside, [whole(old)] + near, after=own_state[1:2])
    across_state = attend("near_across", across, [whole(old)] + near, after=beside_state[1:2])
    (to_across,) = attend("far_across", across, far, across_state, final=True, extra=2, unroll=True)
    from_across = shifted(to_across, 0, 2, 0)
    to_beside = attend("far_beside", beside, far, beside_state, final=True, after=(to_across,), weight=1, unroll=True)
    own_part, weight = attend(
        "far_own", [queries], far, own_state, final=True, after=to_beside[:1], carry=conv_weight, weight=1
    )
    parts = (
        from_across,
        shifted(to_beside[0], 0, -1, 0),
        shifted(to_beside[1], 0, 1, 0),
        own_part,
    )
    hidden, stats = merge(parts, x, w_out, peers)
    down = [(i, i + 1) for i in range(peers - 1)]
    above = lax.ppermute(hidden[tok_count - col_count :], "patch", down)
    below = lax.ppermute(hidden[:col_count], "patch", [(j, i) for i, j in down])
    result = convolve(everyones(stats), hidden, above, below, gn2_gain, weight, time_shift)
    return (result.reshape(row_count, col_count, -1), fresh_keys, fresh_values)


def solution(mesh):
    placed = (
        P(("batch", "patch"), None, None),
        P(),
        P(),
        P(),
        P(),
        P(),
        P(("batch", "patch"), None),
        P(("batch", "patch"), None),
        P(),
        P(),
        P("batch"),
    )
    return jax.shard_map(
        shards,
        mesh=mesh,
        in_specs=placed,
        out_specs=(
            P(("batch", "patch"), None, None),
            P(("batch", "patch"), None),
            P(("batch", "patch"), None),
        ),
        check_vma=False,
    )
```

```python
import functools

import jax
import jax.numpy as jnp
from jax import lax
from jax.experimental import pallas as pl
from jax.experimental.pallas import tpu as pltpu
from jax.sharding import PartitionSpec as P

HEAD = 64
GROUPS = 32
LANES = 128
EXTRA = 32
NY, NZ, NX = 4, 4, 2
EPS = 1e-05
BF = jnp.bfloat16
F32 = jnp.float32


def shifted(x, dy, dz, dx):
    pairs = []
    for y in range(NY):
        for z in range(NZ):
            for c in range(NX):
                to = (((y + dy) % NY) * NZ + (z + dz) % NZ) * NX + (c + dx) % NX
                pairs.append(((y * NZ + z) * NX + c, to))
    return lax.ppermute(x, "patch", pairs)


def members_of(channels, lead, offset):
    width = channels // GROUPS
    shape = (channels, LANES) if lead else (LANES, channels)
    chan = lax.broadcasted_iota(jnp.int32, shape, 0 if lead else 1)
    group = lax.broadcasted_iota(jnp.int32, shape, 1 if lead else 0) - offset
    inside = (chan >= group * width) & (chan < group * width + width)
    return jnp.where(inside, 1.0, 0.0).astype(BF)


def exact_dot(row, ones):
    at = lax.broadcasted_iota(jnp.int32, (16, row.shape[1]), 0)
    rest, cut = row, jnp.zeros((16, row.shape[1]), F32)
    for piece in range(3):
        part = rest.astype(BF).astype(F32)
        rest = rest - part
        cut = jnp.where(at == piece, part, cut)
    return jnp.sum(
        jnp.dot(cut.astype(BF), ones, preferred_element_type=F32), axis=0, keepdims=True
    )


def group_matrices(channels):
    return (
        members_of(channels, True, 0),
        members_of(channels, False, 0),
        members_of(channels, True, GROUPS),
    )


def local_stats(x, peers, matrices):
    rows, channels = x.shape
    count = rows * (channels // GROUPS)
    total = jnp.sum(x, axis=0, keepdims=True)
    mean = exact_dot(total, matrices[0]) / count
    center = exact_dot(mean, matrices[1])
    squares = jnp.sum(jnp.square(x - center), axis=0, keepdims=True)
    spread = exact_dot(squares, matrices[2])
    return jnp.broadcast_to(mean + spread, (peers, LANES))


def combined(stats, channels, count):
    peers = stats.shape[0]
    total = jnp.sum(stats, axis=0, keepdims=True)
    mean = total / peers
    between = jnp.sum(jnp.square(stats - mean), axis=0, keepdims=True) * count
    lead = members_of(channels, False, 0)
    center = exact_dot(mean, lead)
    spread = exact_dot(between, lead) + exact_dot(total, members_of(channels, False, GROUPS))
    return center, lax.rsqrt(spread / (count * peers) + EPS)


def full(shape):
    return pl.BlockSpec(shape, lambda *_: (0,) * len(shape))


HBM = pl.BlockSpec(memory_space=pltpu.HBM)
VMEM = pl.BlockSpec(memory_space=pltpu.VMEM)


def halves(src, dst, sems, first):
    size = src.shape[0] // 2
    return [
        pltpu.make_async_copy(
            src.at[i * size : (i + 1) * size], dst.at[i * size : (i + 1) * size], sems.at[first + i]
        )
        for i in range(2)
    ]


def stats_kernel(x_ref, k_ref, v_ref, wq, wk, wv, out_ref, old_ref, wq_out, wk_out, wv_out, held, sems):
    rows = k_ref.shape[0]
    copies = halves(x_ref, held, sems, 0)
    copies.append(pltpu.make_async_copy(k_ref, old_ref.at[0:rows], sems.at[2]))
    copies.append(pltpu.make_async_copy(v_ref, old_ref.at[rows : 2 * rows], sems.at[3]))
    for i, (src, dst) in enumerate(((wq, wq_out), (wk, wk_out), (wv, wv_out))):
        copies += halves(src, dst, sems, 4 + 2 * i)
    for copy in copies:
        copy.start()
    matrices = group_matrices(x_ref.shape[1])
    for copy in copies[:2]:
        copy.wait()
    out_ref[...] = local_stats(held[...].astype(F32), out_ref.shape[0], matrices)
    for copy in copies[2:]:
        copy.wait()


def norm_stats(x, keys, values, weights, peers):
    rows, width = keys.shape
    return pl.pallas_call(
        stats_kernel,
        in_specs=[HBM] * 6,
        out_specs=[VMEM] * 5,
        out_shape=[
            jax.ShapeDtypeStruct((peers, LANES), F32),
            jax.ShapeDtypeStruct((2 * rows, width), BF),
        ]
        + [pltpu.VMEM(w.shape, w.dtype) for w in weights],
        scratch_shapes=[pltpu.VMEM(x.shape, x.dtype), pltpu.SemaphoreType.DMA((10,))],
        name="norm_stats",
        compiler_params=pltpu.CompilerParams(vmem_limit_bytes=60030976),
        cost_estimate=pl.CostEstimate(flops=4 * x.size, bytes_accessed=2 * x.size, transcendentals=0),
    )(x, keys, values, *weights)


def project_kernel(stats_ref, x_ref, gain_ref, wq, wk, wv, q_ref, k_ref, v_ref, both_ref):
    rows, channels = x_ref.shape
    center, scale = combined(stats_ref[...], channels, rows * (channels // GROUPS))
    gain = gain_ref[...].reshape(1, channels)
    normed = ((x_ref[...].astype(F32) - center) * scale * gain).astype(BF)
    for i, (w_ref, o_ref) in enumerate(((wq, q_ref), (wk, k_ref), (wv, v_ref))):
        found = jnp.dot(normed, w_ref[...], preferred_element_type=F32).astype(BF)
        o_ref[...] = found
        if i > 0:
            both_ref[(i - 1) * rows : i * rows, :] = found


def project(stats, x, gain, wq, wk, wv):
    rows, channels = x.shape
    width = wq.shape[1]
    return pl.pallas_call(
        project_kernel,
        in_specs=[VMEM] * 6,
        out_specs=[VMEM] * 4,
        out_shape=[jax.ShapeDtypeStruct((rows, width), BF)] * 3
        + [jax.ShapeDtypeStruct((2 * rows, width), BF)],
        name="project",
        compiler_params=pltpu.CompilerParams(vmem_limit_bytes=24 * 2**20),
        cost_estimate=pl.CostEstimate(
            flops=6 * rows * channels * width,
            bytes_accessed=6 * channels * width,
            transcendentals=0,
        ),
    )(stats, x, gain, wq, wk, wv)


def scores_of(queries, keys, second):
    lane = lax.broadcasted_iota(jnp.int32, queries.shape, 1)
    mine = jnp.where((lane >= HEAD) if second else (lane < HEAD), queries * BF(0.125), BF(0))
    return lax.dot_general(mine, keys, (((1,), (1,)), ((), ())), preferred_element_type=F32)


def weigh(scores, values):
    top = jnp.max(scores, axis=1, keepdims=True)
    weights = jnp.exp(scores - top).astype(BF)
    both = jnp.dot(weights, values, preferred_element_type=F32)
    return both[:, :LANES], jnp.broadcast_to(top, (scores.shape[0], LANES)), both[:, LANES:]


def attend_kernel(plan, start, final, waits, carry, unroll, *refs):
    count, rows_of = plan
    refs = list(refs)
    take = lambda n: [refs.pop(0) for _ in range(n)]
    queries, sources = take(count), take(2 * len(rows_of))
    state = take(3) if start else None
    take(waits)
    brought = take(1 if carry else 0)
    outs = take(count if final else 3)
    copies = []
    (kept,) = take(1) if carry else (None,)
    (scores,) = take(1)
    (levels,) = take(1) if final else (None,)
    if carry:
        (sems,) = take(1)
        copies = [
            pltpu.make_async_copy(brought[0].at[i], kept.at[i], sems.at[i]) for i in range(kept.shape[0])
        ]
        for copy in copies:
            copy.start()
    rows, width = queries[0].shape
    lane = lax.broadcasted_iota(jnp.int32, (rows, LANES), 1)
    ones = jnp.ones((rows, LANES), BF)
    if final:
        levels[...] = jnp.zeros(levels.shape, F32)
        for o_ref in outs:
            o_ref[rows:, :] = jnp.zeros((o_ref.shape[0] - rows, width), BF)

    pairs = width // LANES
    lanes_of = lambda j: pl.ds(pl.multiple_of(j * LANES, LANES), LANES)
    piece = lambda ref, row, cols: ref[row * rows : (row + 1) * rows, cols]

    def keys_of(cols):
        return jnp.concatenate([piece(sources[2 * i], r, cols) for i, (r, _) in enumerate(rows_of)])

    def values_of(cols):
        found = [piece(sources[2 * i + 1], r, cols) for i, (_, r) in enumerate(rows_of)]
        return jnp.concatenate([jnp.concatenate([v, ones], axis=1) for v in found])

    def step(j, following):
        cols = lanes_of(j)
        values = values_of(cols)
        if following:
            later = lanes_of(j + 1)
            keys = keys_of(later)
        for band, q_ref in enumerate(queries):
            found = []
            for h in range(2):
                found.append(weigh(scores[2 * band + h], values))
                if following:
                    scores[2 * band + h] = scores_of(q_ref[:, later], keys, h)
            first = lane < HEAD
            at = slice(band * rows, (band + 1) * rows)
            summed, top, total = (jnp.where(first, found[0][n], found[1][n]) for n in range(3))
            if state is not None:
                old_top = state[1][at, cols]
                new_top = jnp.maximum(top, old_top)
                part, old_part = jnp.exp(top - new_top), jnp.exp(old_top - new_top)
                top = new_top
                total = part * total + old_part * state[2][at, cols]
                summed = part * summed + old_part * state[0][at, cols]
            if not final:
                for out_ref, value in zip(outs, (summed, top, total)):
                    out_ref[at, cols] = value
                continue
            outs[band][0:rows, cols] = (summed / total).astype(BF)
            level = top + jnp.log(total)
            turned = level.T
            for h in range(2):
                rest = turned[h * HEAD : h * HEAD + 1, :]
                for cut in range(3):
                    part = rest.astype(BF).astype(F32)
                    rest = rest - part
                    levels[band, pl.ds(10 * cut + 2 * j + h, 1), :] = part

    start_keys = keys_of(slice(0, LANES))
    for band, q_ref in enumerate(queries):
        for h in range(2):
            scores[2 * band + h] = scores_of(q_ref[:, 0:LANES], start_keys, h)

    def loop_step(j, carried):
        step(j, True)
        return carried

    lax.fori_loop(0, pairs - 1, loop_step, 0, unroll=unroll)
    step(pairs - 1, False)
    if final:
        for band, o_ref in enumerate(outs):
            o_ref[rows : rows + EXTRA, 0:rows] = levels[band].astype(BF)
    for copy in copies:
        copy.wait()


def attend(name, queries, blocks, state=None, final=False, after=(), carry=None, weight=16, extra=0, unroll=False):
    rows, width = queries[0].shape
    count = len(queries)
    sources = []
    for keys, _, values, _ in blocks:
        sources += [keys, values]
    plan = (count, [(key_row, value_row) for _, key_row, _, value_row in blocks])
    if final:
        out_shape = [jax.ShapeDtypeStruct((rows + EXTRA + extra, width), BF)] * count
    else:
        out_shape = [jax.ShapeDtypeStruct((count * rows, width), F32)] * 3
    scratch = [pltpu.VMEM((2 * count, rows, len(blocks) * rows), F32)]
    if final:
        scratch.append(pltpu.VMEM((count, EXTRA, rows), F32))
    carried = []
    if carry is not None:
        out_shape.append(pltpu.VMEM(carry.shape, carry.dtype))
        scratch.append(pltpu.SemaphoreType.DMA((carry.shape[0],)))
        carried.append(carry)
    state = tuple(state or ())
    return pl.pallas_call(
        functools.partial(attend_kernel, plan, bool(state), final, len(after), carry is not None, unroll),
        in_specs=[VMEM] * (count + len(sources) + len(state))
        + [pl.BlockSpec(memory_space=pl.ANY)] * len(after)
        + [HBM] * len(carried),
        out_specs=[VMEM] * len(out_shape),
        out_shape=out_shape,
        scratch_shapes=scratch,
        name=name,
        compiler_params=pltpu.CompilerParams(vmem_limit_bytes=24 * 2**20),
        cost_estimate=pl.CostEstimate(
            flops=weight * count * rows * len(blocks) * rows * width,
            bytes_accessed=weight * rows * LANES,
            transcendentals=0,
        ),
    )(*queries, *sources, *state, *after, *carried)


def merge_kernel(p0, p1, p2, p3, x_ref, w_ref, hidden_ref, stats_ref):
    width = w_ref.shape[0]
    rows = x_ref.shape[0]
    row = lax.broadcasted_iota(jnp.int32, (EXTRA, width), 0)
    chan = lax.broadcasted_iota(jnp.int32, (EXTRA, width), 1)
    spread = jnp.zeros((EXTRA, width), F32)
    for cut in range(3):
        head = row - 10 * cut
        inside = (head >= 0) & (head < 10) & (chan >= head * HEAD) & (chan < head * HEAD + HEAD)
        spread = jnp.where(inside, 1.0, spread)
    spread = spread.astype(BF)
    parts = (p0, p1, p2, p3)
    levels = [
        lax.dot_general(
            p[rows : rows + EXTRA, 0:rows], spread, (((0,), (0,)), ((), ())), preferred_element_type=F32
        )
        for p in parts
    ]
    top = functools.reduce(jnp.maximum, levels)
    shares = [jnp.exp(level - top) for level in levels]
    total = functools.reduce(jnp.add, shares)
    summed = functools.reduce(
        jnp.add, [s * p[0:rows, :].astype(F32) for s, p in zip(shares, parts)]
    )
    attended = (summed / total).astype(BF)
    hidden = x_ref[...].astype(F32) + jnp.dot(attended, w_ref[...], preferred_element_type=F32)
    hidden_ref[...] = hidden
    stats_ref[...] = local_stats(hidden, stats_ref.shape[0], group_matrices(hidden.shape[1]))


def merge(parts, x, w_out, peers):
    rows, channels = x.shape
    return pl.pallas_call(
        merge_kernel,
        out_shape=[
            jax.ShapeDtypeStruct((rows, channels), F32),
            jax.ShapeDtypeStruct((peers, LANES), F32),
        ],
        name="merge_project",
        compiler_params=pltpu.CompilerParams(vmem_limit_bytes=24 * 2**20),
        cost_estimate=pl.CostEstimate(
            flops=2 * rows * w_out.size, bytes_accessed=2 * w_out.size, transcendentals=0
        ),
    )(*parts, x, w_out)


def conv_kernel(stats_ref, hidden_ref, above_ref, below_ref, gain_ref, w_ref, shift_ref, out_ref, moved):
    own = lax.axis_index("patch")
    last = lax.axis_size("patch") - 1
    rows, channels = hidden_ref.shape
    cols = above_ref.shape[0]
    width = out_ref.shape[1]
    center, scale = combined(stats_ref[...], channels, rows * (channels // GROUPS))
    scale = 0.5 * scale * gain_ref[...].reshape(1, channels)
    col = lax.broadcasted_iota(jnp.int32, (cols, channels), 0)
    pieces = [(above_ref, 0, own != 0)]
    pieces += [(hidden_ref, i, None) for i in range(rows // cols)]
    pieces += [(below_ref, 0, own != last)]
    for place, (ref, part, kept) in enumerate(pieces):
        half = (ref[part * cols : (part + 1) * cols, :] - center) * scale
        v = half * jnp.tanh(half) + half
        if kept is not None:
            v = jnp.where(kept, v, 0.0)
        to = slice(place * cols, (place + 1) * cols)
        left = jnp.where(col == 0, 0.0, pltpu.roll(v, 1, 0))
        right = jnp.where(col == cols - 1, 0.0, pltpu.roll(v, cols - 1, 0))
        for tap, value in enumerate((left, v, right)):
            moved[to, tap * channels : (tap + 1) * channels] = value.astype(BF)
    total = hidden_ref[:, :width] + shift_ref[...].reshape(1, width)
    for tap in range(3):
        window = moved[tap * cols : tap * cols + rows, :]
        taps = w_ref[3 * tap : 3 * tap + 3].reshape(3 * channels, width)
        total = total + jnp.dot(window, taps, preferred_element_type=F32)
    out_ref[...] = total.astype(BF)


def convolve(stats, hidden, above, below, gain, weight, shift):
    rows, channels = hidden.shape
    cols = above.shape[0]
    width = weight.shape[2]
    return pl.pallas_call(
        conv_kernel,
        in_specs=[VMEM] * 7,
        out_specs=VMEM,
        out_shape=jax.ShapeDtypeStruct((rows, width), BF),
        scratch_shapes=[pltpu.VMEM((rows + 2 * cols, 3 * channels), BF)],
        name="norm_convolve",
        compiler_params=pltpu.CompilerParams(vmem_limit_bytes=24 * 2**20),
        cost_estimate=pl.CostEstimate(
            flops=2 * rows * weight.size, bytes_accessed=2 * weight.size, transcendentals=0
        ),
    )(stats, hidden, above, below, gain, weight, shift)


def everyones(stats):
    return lax.all_to_all(stats, "patch", 0, 0, tiled=True)


def shards(
    latent,
    gn_gain,
    w_query,
    w_key,
    w_value,
    w_out,
    stale_keys,
    stale_values,
    gn2_gain,
    conv_weight,
    time_shift,
):
    row_count, col_count, channels = latent.shape
    tok_count = row_count * col_count
    peers = lax.axis_size("patch")
    x = latent.reshape(tok_count, channels)
    stats, old, *weights = norm_stats(x, stale_keys, stale_values, (w_query, w_key, w_value), peers)
    from_below = shifted(old, 1, 0, 0)
    from_above = shifted(old, -1, 0, 0)
    from_side = shifted(old, 0, 0, 1)
    stats = everyones(stats)
    queries, fresh_keys, fresh_values, fresh = project(stats, x, gn_gain, *weights)

    relayed, _ = lax.optimization_barrier((from_side, stats))
    side_below = shifted(relayed, 1, 0, 0)
    side_above = shifted(relayed, -1, 0, 0)
    beside = [shifted(queries, 0, 1, 0), shifted(queries, 0, -1, 0)]
    across = [shifted(queries, 0, 2, 0)]
    last_keys = shifted(jnp.concatenate([from_below[:tok_count], side_below[:tok_count]]), 1, 0, 0)
    last_values = shifted(jnp.concatenate([from_above[tok_count:], side_above[tok_count:]]), -1, 0, 0)

    whole = lambda block: (block, 0, block, 1)
    near = [whole(from_below), whole(from_above), whole(from_side)]
    far = [whole(side_below), whole(side_above)]
    far += [(last_keys, 0, last_values, 0), (last_keys, 1, last_values, 1)]
    own_state = attend("near_own", [queries], [whole(fresh)] + near)
    beside_state = attend("near_beside", beside, [whole(old)] + near, after=own_state[1:2])
    across_state = attend("near_across", across, [whole(old)] + near, after=beside_state[1:2], unroll=True)
    (to_across,) = attend("far_across", across, far, across_state, final=True, extra=16, unroll=True)
    from_across = shifted(to_across, 0, 2, 0)
    to_beside = attend("far_beside", beside, far, beside_state, final=True, after=(to_across,), weight=1, unroll=True)
    own_part, weight = attend(
        "far_own", [queries], far, own_state, final=True, after=to_beside[:1], carry=conv_weight, weight=1
    )
    parts = (
        from_across,
        shifted(to_beside[0], 0, -1, 0),
        shifted(to_beside[1], 0, 1, 0),
        own_part,
    )
    hidden, stats = merge(parts, x, w_out, peers)
    down = [(i, i + 1) for i in range(peers - 1)]
    above = lax.ppermute(hidden[tok_count - col_count :], "patch", down)
    below = lax.ppermute(hidden[:col_count], "patch", [(j, i) for i, j in down])
    result = convolve(everyones(stats), hidden, above, below, gn2_gain, weight, time_shift)
    return (result.reshape(row_count, col_count, -1), fresh_keys, fresh_values)


def solution(mesh):
    placed = (
        P(("batch", "patch"), None, None),
        P(),
        P(),
        P(),
        P(),
        P(),
        P(("batch", "patch"), None),
        P(("batch", "patch"), None),
        P(),
        P(),
        P("batch"),
    )
    return jax.shard_map(
        shards,
        mesh=mesh,
        in_specs=placed,
        out_specs=(
            P(("batch", "patch"), None, None),
            P(("batch", "patch"), None),
            P(("batch", "patch"), None),
        ),
        check_vma=False,
    )
```

```python
import functools

import jax
import jax.numpy as jnp
from jax import lax
from jax.experimental import pallas as pl
from jax.experimental.pallas import tpu as pltpu
from jax.sharding import PartitionSpec as P

HEAD = 64
GROUPS = 32
LANES = 128
EXTRA = 32
NY, NZ, NX = 4, 4, 2
EPS = 1e-05
BF = jnp.bfloat16
F32 = jnp.float32


def shifted(x, dy, dz, dx):
    pairs = []
    for y in range(NY):
        for z in range(NZ):
            for c in range(NX):
                to = (((y + dy) % NY) * NZ + (z + dz) % NZ) * NX + (c + dx) % NX
                pairs.append(((y * NZ + z) * NX + c, to))
    return lax.ppermute(x, "patch", pairs)


def members_of(channels, lead, offset):
    width = channels // GROUPS
    shape = (channels, LANES) if lead else (LANES, channels)
    chan = lax.broadcasted_iota(jnp.int32, shape, 0 if lead else 1)
    group = lax.broadcasted_iota(jnp.int32, shape, 1 if lead else 0) - offset
    inside = (chan >= group * width) & (chan < group * width + width)
    return jnp.where(inside, 1.0, 0.0).astype(BF)


def exact_dots(rows, ones):
    at = lax.broadcasted_iota(jnp.int32, (16, rows[0].shape[1]), 0)
    cut = jnp.zeros(at.shape, F32)
    for i, rest in enumerate(rows):
        for piece in range(3):
            part = rest.astype(BF).astype(F32)
            rest = rest - part
            cut = jnp.where(at == 8 * i + piece, part, cut)
    found = jnp.dot(cut.astype(BF), ones, preferred_element_type=F32)
    return [jnp.sum(found[8 * i : 8 * i + 8], axis=0, keepdims=True) for i in range(len(rows))]


def exact_dot(row, ones):
    return exact_dots([row], ones)[0]


def group_matrices(channels):
    return (
        members_of(channels, True, 0),
        members_of(channels, False, 0),
        members_of(channels, True, GROUPS),
    )


def local_stats(x, peers, matrices):
    rows, channels = x.shape
    count = rows * (channels // GROUPS)
    total = jnp.sum(x, axis=0, keepdims=True)
    mean = exact_dot(total, matrices[0]) / count
    center = exact_dot(mean, matrices[1])
    squares = jnp.sum(jnp.square(x - center), axis=0, keepdims=True)
    spread = exact_dot(squares, matrices[2])
    return jnp.broadcast_to(mean + spread, (peers, LANES))


def combined(stats, channels, count):
    peers = stats.shape[0]
    total = jnp.sum(stats, axis=0, keepdims=True)
    mean = total / peers
    between = jnp.sum(jnp.square(stats - mean), axis=0, keepdims=True) * count
    lane = lax.broadcasted_iota(jnp.int32, mean.shape, 1)
    both = members_of(channels, False, 0) + members_of(channels, False, GROUPS)
    center, spread = exact_dots(
        [jnp.where(lane < GROUPS, mean, 0.0), jnp.where(lane < GROUPS, between, total)], both
    )
    return center, lax.rsqrt(spread / (count * peers) + EPS)


def full(shape):
    return pl.BlockSpec(shape, lambda *_: (0,) * len(shape))


HBM = pl.BlockSpec(memory_space=pltpu.HBM)
VMEM = pl.BlockSpec(memory_space=pltpu.VMEM)


def halves(src, dst, sems, first):
    size = src.shape[0] // 2
    return [
        pltpu.make_async_copy(
            src.at[i * size : (i + 1) * size], dst.at[i * size : (i + 1) * size], sems.at[first + i]
        )
        for i in range(2)
    ]


def stats_kernel(x_ref, k_ref, v_ref, wq, wk, wv, out_ref, old_ref, wq_out, wk_out, wv_out, held, sems):
    rows = k_ref.shape[0]
    copies = halves(x_ref, held, sems, 0)
    copies.append(pltpu.make_async_copy(k_ref, old_ref.at[0:rows], sems.at[2]))
    copies.append(pltpu.make_async_copy(v_ref, old_ref.at[rows : 2 * rows], sems.at[3]))
    for i, (src, dst) in enumerate(((wq, wq_out), (wk, wk_out), (wv, wv_out))):
        copies += halves(src, dst, sems, 4 + 2 * i)
    for copy in copies:
        copy.start()
    matrices = group_matrices(x_ref.shape[1])
    for copy in copies[:2]:
        copy.wait()
    out_ref[...] = local_stats(held[...].astype(F32), out_ref.shape[0], matrices)
    for copy in copies[2:]:
        copy.wait()


def norm_stats(x, keys, values, weights, peers):
    rows, width = keys.shape
    return pl.pallas_call(
        stats_kernel,
        in_specs=[HBM] * 6,
        out_specs=[VMEM] * 5,
        out_shape=[
            jax.ShapeDtypeStruct((peers, LANES), F32),
            jax.ShapeDtypeStruct((2 * rows, width), BF),
        ]
        + [pltpu.VMEM(w.shape, w.dtype) for w in weights],
        scratch_shapes=[pltpu.VMEM(x.shape, x.dtype), pltpu.SemaphoreType.DMA((10,))],
        name="norm_stats",
        compiler_params=pltpu.CompilerParams(vmem_limit_bytes=60030976),
        cost_estimate=pl.CostEstimate(flops=4 * x.size, bytes_accessed=2 * x.size, transcendentals=0),
    )(x, keys, values, *weights)


def project_kernel(stats_ref, x_ref, gain_ref, wq, wk, wv, q_ref, k_ref, v_ref, both_ref):
    rows, channels = x_ref.shape
    center, scale = combined(stats_ref[...], channels, rows * (channels // GROUPS))
    gain = gain_ref[...].reshape(1, channels)
    normed = ((x_ref[...].astype(F32) - center) * scale * gain).astype(BF)
    for i, (w_ref, o_ref) in enumerate(((wq, q_ref), (wk, k_ref), (wv, v_ref))):
        found = jnp.dot(normed, w_ref[...], preferred_element_type=F32).astype(BF)
        o_ref[...] = found
        if i > 0:
            both_ref[(i - 1) * rows : i * rows, :] = found


def project(stats, x, gain, wq, wk, wv):
    rows, channels = x.shape
    width = wq.shape[1]
    return pl.pallas_call(
        project_kernel,
        in_specs=[VMEM] * 6,
        out_specs=[VMEM] * 4,
        out_shape=[jax.ShapeDtypeStruct((rows, width), BF)] * 3
        + [jax.ShapeDtypeStruct((2 * rows, width), BF)],
        name="project",
        compiler_params=pltpu.CompilerParams(vmem_limit_bytes=24 * 2**20),
        cost_estimate=pl.CostEstimate(
            flops=6 * rows * channels * width,
            bytes_accessed=6 * channels * width,
            transcendentals=0,
        ),
    )(stats, x, gain, wq, wk, wv)


def scores_of(queries, keys, second):
    lane = lax.broadcasted_iota(jnp.int32, queries.shape, 1)
    mine = jnp.where((lane >= HEAD) if second else (lane < HEAD), queries * BF(0.125), BF(0))
    return lax.dot_general(mine, keys, (((1,), (1,)), ((), ())), preferred_element_type=F32)


def weigh(scores, values):
    top = jnp.max(scores, axis=1, keepdims=True)
    weights = jnp.exp(scores - top).astype(BF)
    both = jnp.dot(weights, values, preferred_element_type=F32)
    return both[:, :LANES], jnp.broadcast_to(top, (scores.shape[0], LANES)), both[:, LANES:]


def attend_kernel(plan, start, final, waits, carry, unroll, *refs):
    count, rows_of = plan
    refs = list(refs)
    take = lambda n: [refs.pop(0) for _ in range(n)]
    queries, sources = take(count), take(2 * len(rows_of))
    state = take(3) if start else None
    take(waits)
    brought = take(1 if carry else 0)
    outs = take(count if final else 3)
    copies = []
    (kept,) = take(1) if carry else (None,)
    (scores,) = take(1)
    (levels,) = take(1) if final else (None,)
    if carry:
        (sems,) = take(1)
        copies = [
            pltpu.make_async_copy(brought[0].at[i], kept.at[i], sems.at[i]) for i in range(kept.shape[0])
        ]
        for copy in copies:
            copy.start()
    rows, width = queries[0].shape
    lane = lax.broadcasted_iota(jnp.int32, (rows, LANES), 1)
    ones = jnp.ones((rows, LANES), BF)
    if final:
        levels[...] = jnp.zeros(levels.shape, F32)
        for o_ref in outs:
            o_ref[rows:, :] = jnp.zeros((o_ref.shape[0] - rows, width), BF)

    pairs = width // LANES
    lanes_of = lambda j: pl.ds(pl.multiple_of(j * LANES, LANES), LANES)
    piece = lambda ref, row, cols: ref[row * rows : (row + 1) * rows, cols]

    def keys_of(cols):
        return jnp.concatenate([piece(sources[2 * i], r, cols) for i, (r, _) in enumerate(rows_of)])

    def values_of(cols):
        found = [piece(sources[2 * i + 1], r, cols) for i, (_, r) in enumerate(rows_of)]
        return jnp.concatenate([jnp.concatenate([v, ones], axis=1) for v in found])

    def step(j, following):
        cols = lanes_of(j)
        values = values_of(cols)
        if following:
            later = lanes_of(j + 1)
            keys = keys_of(later)
        for band, q_ref in enumerate(queries):
            found = []
            for h in range(2):
                found.append(weigh(scores[2 * band + h], values))
                if following:
                    scores[2 * band + h] = scores_of(q_ref[:, later], keys, h)
            first = lane < HEAD
            at = slice(band * rows, (band + 1) * rows)
            summed, top, total = (jnp.where(first, found[0][n], found[1][n]) for n in range(3))
            if state is not None:
                old_top = state[1][at, cols]
                new_top = jnp.maximum(top, old_top)
                part, old_part = jnp.exp(top - new_top), jnp.exp(old_top - new_top)
                top = new_top
                total = part * total + old_part * state[2][at, cols]
                summed = part * summed + old_part * state[0][at, cols]
            if not final:
                for out_ref, value in zip(outs, (summed, top, total)):
                    out_ref[at, cols] = value
                continue
            outs[band][0:rows, cols] = (summed / total).astype(BF)
            level = top + jnp.log(total)
            turned = level.T
            for h in range(2):
                rest = turned[h * HEAD : h * HEAD + 1, :]
                for cut in range(3):
                    part = rest.astype(BF).astype(F32)
                    rest = rest - part
                    levels[band, pl.ds(10 * cut + 2 * j + h, 1), :] = part

    start_keys = keys_of(slice(0, LANES))
    for band, q_ref in enumerate(queries):
        for h in range(2):
            scores[2 * band + h] = scores_of(q_ref[:, 0:LANES], start_keys, h)

    def loop_step(j, carried):
        step(j, True)
        return carried

    lax.fori_loop(0, pairs - 1, loop_step, 0, unroll=unroll)
    step(pairs - 1, False)
    if final:
        for band, o_ref in enumerate(outs):
            o_ref[rows : rows + EXTRA, 0:rows] = levels[band].astype(BF)
    for copy in copies:
        copy.wait()


def attend(name, queries, blocks, state=None, final=False, after=(), carry=None, weight=16, extra=0, unroll=False):
    rows, width = queries[0].shape
    count = len(queries)
    sources = []
    for keys, _, values, _ in blocks:
        sources += [keys, values]
    plan = (count, [(key_row, value_row) for _, key_row, _, value_row in blocks])
    if final:
        out_shape = [jax.ShapeDtypeStruct((rows + EXTRA + extra, width), BF)] * count
    else:
        out_shape = [jax.ShapeDtypeStruct((count * rows, width), F32)] * 3
    scratch = [pltpu.VMEM((2 * count, rows, len(blocks) * rows), F32)]
    if final:
        scratch.append(pltpu.VMEM((count, EXTRA, rows), F32))
    carried = []
    if carry is not None:
        out_shape.append(pltpu.VMEM(carry.shape, carry.dtype))
        scratch.append(pltpu.SemaphoreType.DMA((carry.shape[0],)))
        carried.append(carry)
    state = tuple(state or ())
    return pl.pallas_call(
        functools.partial(attend_kernel, plan, bool(state), final, len(after), carry is not None, unroll),
        in_specs=[VMEM] * (count + len(sources) + len(state))
        + [pl.BlockSpec(memory_space=pl.ANY)] * len(after)
        + [HBM] * len(carried),
        out_specs=[VMEM] * len(out_shape),
        out_shape=out_shape,
        scratch_shapes=scratch,
        name=name,
        compiler_params=pltpu.CompilerParams(vmem_limit_bytes=24 * 2**20),
        cost_estimate=pl.CostEstimate(
            flops=weight * count * rows * len(blocks) * rows * width,
            bytes_accessed=weight * rows * LANES,
            transcendentals=0,
        ),
    )(*queries, *sources, *state, *after, *carried)


def merge_kernel(p0, p1, p2, p3, x_ref, w_ref, hidden_ref, stats_ref):
    width = w_ref.shape[0]
    rows = x_ref.shape[0]
    row = lax.broadcasted_iota(jnp.int32, (EXTRA, width), 0)
    chan = lax.broadcasted_iota(jnp.int32, (EXTRA, width), 1)
    spread = jnp.zeros((EXTRA, width), F32)
    for cut in range(3):
        head = row - 10 * cut
        inside = (head >= 0) & (head < 10) & (chan >= head * HEAD) & (chan < head * HEAD + HEAD)
        spread = jnp.where(inside, 1.0, spread)
    spread = spread.astype(BF)
    parts = (p0, p1, p2, p3)
    levels = [
        lax.dot_general(
            p[rows : rows + EXTRA, 0:rows], spread, (((0,), (0,)), ((), ())), preferred_element_type=F32
        )
        for p in parts
    ]
    top = functools.reduce(jnp.maximum, levels)
    shares = [jnp.exp(level - top) for level in levels]
    total = functools.reduce(jnp.add, shares)
    summed = functools.reduce(
        jnp.add, [s * p[0:rows, :].astype(F32) for s, p in zip(shares, parts)]
    )
    attended = (summed / total).astype(BF)
    hidden = x_ref[...].astype(F32) + jnp.dot(attended, w_ref[...], preferred_element_type=F32)
    hidden_ref[...] = hidden
    stats_ref[...] = local_stats(hidden, stats_ref.shape[0], group_matrices(hidden.shape[1]))


def merge(parts, x, w_out, peers):
    rows, channels = x.shape
    return pl.pallas_call(
        merge_kernel,
        out_shape=[
            jax.ShapeDtypeStruct((rows, channels), F32),
            jax.ShapeDtypeStruct((peers, LANES), F32),
        ],
        name="merge_project",
        compiler_params=pltpu.CompilerParams(vmem_limit_bytes=24 * 2**20),
        cost_estimate=pl.CostEstimate(
            flops=2 * rows * w_out.size, bytes_accessed=2 * w_out.size, transcendentals=0
        ),
    )(*parts, x, w_out)


def conv_kernel(stats_ref, hidden_ref, above_ref, below_ref, gain_ref, w_ref, shift_ref, out_ref, moved):
    own = lax.axis_index("patch")
    last = lax.axis_size("patch") - 1
    rows, channels = hidden_ref.shape
    cols = above_ref.shape[0]
    width = out_ref.shape[1]
    center, scale = combined(stats_ref[...], channels, rows * (channels // GROUPS))
    scale = 0.5 * scale * gain_ref[...].reshape(1, channels)
    col = lax.broadcasted_iota(jnp.int32, (cols, channels), 0)
    pieces = [(above_ref, 0, own != 0)]
    pieces += [(hidden_ref, i, None) for i in range(rows // cols)]
    pieces += [(below_ref, 0, own != last)]
    for place, (ref, part, kept) in enumerate(pieces):
        half = (ref[part * cols : (part + 1) * cols, :] - center) * scale
        v = half * jnp.tanh(half) + half
        if kept is not None:
            v = jnp.where(kept, v, 0.0)
        to = slice(place * cols, (place + 1) * cols)
        left = jnp.where(col == 0, 0.0, pltpu.roll(v, 1, 0))
        right = jnp.where(col == cols - 1, 0.0, pltpu.roll(v, cols - 1, 0))
        for tap, value in enumerate((left, v, right)):
            moved[to, tap * channels : (tap + 1) * channels] = value.astype(BF)
    total = hidden_ref[:, :width] + shift_ref[...].reshape(1, width)
    for tap in range(3):
        window = moved[tap * cols : tap * cols + rows, :]
        taps = w_ref[3 * tap : 3 * tap + 3].reshape(3 * channels, width)
        total = total + jnp.dot(window, taps, preferred_element_type=F32)
    out_ref[...] = total.astype(BF)


def convolve(stats, hidden, above, below, gain, weight, shift):
    rows, channels = hidden.shape
    cols = above.shape[0]
    width = weight.shape[2]
    return pl.pallas_call(
        conv_kernel,
        in_specs=[VMEM] * 7,
        out_specs=VMEM,
        out_shape=jax.ShapeDtypeStruct((rows, width), BF),
        scratch_shapes=[pltpu.VMEM((rows + 2 * cols, 3 * channels), BF)],
        name="norm_convolve",
        compiler_params=pltpu.CompilerParams(vmem_limit_bytes=24 * 2**20),
        cost_estimate=pl.CostEstimate(
            flops=2 * rows * weight.size, bytes_accessed=2 * weight.size, transcendentals=0
        ),
    )(stats, hidden, above, below, gain, weight, shift)


def everyones(stats):
    return lax.all_to_all(stats, "patch", 0, 0, tiled=True)


def shards(
    latent,
    gn_gain,
    w_query,
    w_key,
    w_value,
    w_out,
    stale_keys,
    stale_values,
    gn2_gain,
    conv_weight,
    time_shift,
):
    row_count, col_count, channels = latent.shape
    tok_count = row_count * col_count
    peers = lax.axis_size("patch")
    x = latent.reshape(tok_count, channels)
    stats, old, *weights = norm_stats(x, stale_keys, stale_values, (w_query, w_key, w_value), peers)
    from_below = shifted(old, 1, 0, 0)
    from_above = shifted(old, -1, 0, 0)
    from_side = shifted(old, 0, 0, 1)
    stats = everyones(stats)
    queries, fresh_keys, fresh_values, fresh = project(stats, x, gn_gain, *weights)

    relayed, _ = lax.optimization_barrier((from_side, stats))
    side_below = shifted(relayed, 1, 0, 0)
    side_above = shifted(relayed, -1, 0, 0)
    beside = [shifted(queries, 0, 1, 0), shifted(queries, 0, -1, 0)]
    across = [shifted(queries, 0, 2, 0)]
    last_keys = shifted(jnp.concatenate([from_below[:tok_count], side_below[:tok_count]]), 1, 0, 0)
    last_values = shifted(jnp.concatenate([from_above[tok_count:], side_above[tok_count:]]), -1, 0, 0)

    whole = lambda block: (block, 0, block, 1)
    near = [whole(from_below), whole(from_above), whole(from_side)]
    far = [whole(side_below), whole(side_above)]
    far += [(last_keys, 0, last_values, 0), (last_keys, 1, last_values, 1)]
    own_state = attend("near_own", [queries], [whole(fresh)] + near)
    beside_state = attend("near_beside", beside, [whole(old)] + near, after=own_state[1:2])
    across_state = attend("near_across", across, [whole(old)] + near, after=beside_state[1:2], unroll=True)
    (to_across,) = attend("far_across", across, far, across_state, final=True, extra=16, unroll=True)
    from_across = shifted(to_across, 0, 2, 0)
    to_beside = attend("far_beside", beside, far, beside_state, final=True, after=(to_across,), weight=1, unroll=True)
    own_part, weight = attend(
        "far_own", [queries], far, own_state, final=True, after=to_beside[:1], carry=conv_weight, weight=1
    )
    parts = (
        from_across,
        shifted(to_beside[0], 0, -1, 0),
        shifted(to_beside[1], 0, 1, 0),
        own_part,
    )
    hidden, stats = merge(parts, x, w_out, peers)
    down = [(i, i + 1) for i in range(peers - 1)]
    above = lax.ppermute(hidden[tok_count - col_count :], "patch", down)
    below = lax.ppermute(hidden[:col_count], "patch", [(j, i) for i, j in down])
    result = convolve(everyones(stats), hidden, above, below, gn2_gain, weight, time_shift)
    return (result.reshape(row_count, col_count, -1), fresh_keys, fresh_values)


def solution(mesh):
    placed = (
        P(("batch", "patch"), None, None),
        P(),
        P(),
        P(),
        P(),
        P(),
        P(("batch", "patch"), None),
        P(("batch", "patch"), None),
        P(),
        P(),
        P("batch"),
    )
    return jax.shard_map(
        shards,
        mesh=mesh,
        in_specs=placed,
        out_specs=(
            P(("batch", "patch"), None, None),
            P(("batch", "patch"), None),
            P(("batch", "patch"), None),
        ),
        check_vma=False,
    )
```
